128 devices in a mesh: unit: 2 (over y_lo), pool: 64 (over z, x, y_hi, core).
Axes of the slice: x: 4, y: 4 (y_hi: 2, y_lo: 2; y = y_hi * 2 + y_lo), z: 4, core: 2. Of those that a mesh axis runs over, the one named last changes fastest.
Arguments:
- hidden_in: bfloat16 [128, 8192], P('unit', 'pool'), parts along dimension 0
- attn_gain: bfloat16 [8192], P('pool'), may hold values from 0.5 to 1.5
- w_query: bfloat16 [8192, 4096], P('pool'), may hold values from -0.0625 to 0.0625
- key_value_weight: bfloat16 [8192, 1024], P('pool'), may hold values from -0.25 to 0.25
- w_out: bfloat16 [4096, 8192], P(None, 'pool'), may hold values from -0.1875 to 0.1875
- ffn_gain: bfloat16 [8192], replicated, may hold values from 0.5 to 1.5
- w_gate: bfloat16 [8192, 16384], P(None, 'pool'), may hold values from -0.0625 to 0.0625
- w_up: bfloat16 [8192, 16384], P(None, 'pool'), may hold values from -0.0625 to 0.0625
- w_down: bfloat16 [16384, 8192], P('pool'), may hold values from -0.09375 to 0.09375
- cached_key_slots: bfloat16 [655360, 512], P(('unit', 'pool')), parts along dimension 0
- cached_value_slots: bfloat16 [655360, 512], P(('unit', 'pool')), parts along dimension 0, may hold values from -6 to 6
- lengths: int32 [128], P('unit'), parts along dimension 0, may hold values from 1024 to 5120, as said below
- home_device: int32 [128], P('unit'), parts along dimension 0, may hold values from 0 to 63, as said below
- offset: int32 [128], P('unit'), parts along dimension 0, may hold values from 0 to 4097, as said below
Outputs:
- hidden_out: bfloat16 [128, 8192], P('unit', 'pool'), parts along dimension 0
The draws below stay inside these ranges and needn't reach their ends.
There are 2 independent parts, one for each index of `unit`. The reference program is written for one: setup_inputs(seed, part) draws one part's arguments, and reference() takes and returns one part's arrays. A program takes and returns all parts, laid end to end along the dimension named above; an argument that names none is the same for every part. Nothing has to cross between parts.
Inputs may be any that keep to these rules, and one draw needn't show every extreme that they name: `lengths`: A request whose device holds k requests has at most 5120 // k; one request has exactly 5120 and one exactly 1024. `home_device`: in some order the devices hold 4, 3, 2 and 2 requests, then 64 - 11 devices one each, and the other seven none. `offset`: the requests of one device occupy disjoint runs of lengths - 1 slots within its 5120 slots, in row order.
All inputs are finite; a program needn't handle non-finite values.
Results may differ from the reference program's by a relative error of at most 0.015.
Values may be sent and summed in bfloat16 or wider, within the bound.
A program may use at most 128 MiB of HBM per device.

```python
import math
import jax
import jax.numpy as jnp
from jax import lax

MODEL_DIM = 8192
QUERY_HEADS = 32
KEY_VALUE_HEADS = 4
HEAD_DIM = 128
FF = 16384
MAXLEN = 5120
MINLEN = 1024
SLOT_CAPACITY = 5120
ROWS = 64
N_POOL = 64


def request_layout(key):
    position = jnp.arange(ROWS, dtype=jnp.int32)
    bucket = jnp.where(position < 4, 0, jnp.where(position < 7, 1, jnp.where(position < 9, 2, jnp.where(position < 11, 3, position - 7))))
    load = jnp.where(bucket == 0, 4, jnp.where(bucket == 1, 3, jnp.where(bucket < 4, 2, 1)))
    devices = jax.random.permutation(jax.random.fold_in(key, 11), ROWS)
    order = jax.random.permutation(jax.random.fold_in(key, 12), ROWS)
    holder = devices[bucket][order]
    load = load[order]
    position = position[order]
    ceiling = MAXLEN // load
    length = jax.random.randint(jax.random.fold_in(key, 13), (ROWS,), MINLEN, ceiling + 1)
    length = jnp.where(position == 11, MAXLEN, jnp.where(position == 0, MINLEN, length))
    past = length - 1
    same = holder[:, None] == holder[None, :]
    row_ids = jnp.arange(ROWS, dtype=jnp.int32)
    used = jnp.sum(jnp.where(same, past[None, :], 0), axis=1)
    before = jnp.sum(jnp.where(same & (row_ids[None, :] < row_ids[:, None]), past[None, :], 0), axis=1)
    spare = jax.random.randint(jax.random.fold_in(key, 14), (ROWS,), 0, SLOT_CAPACITY + 1)[holder]
    start = spare % (SLOT_CAPACITY - used + 1) + before
    return (holder.astype(jnp.int32), length.astype(jnp.int32), start.astype(jnp.int32))


def draw_home_device(key, part):
    return request_layout(key)[0]


def draw_lengths(key, part):
    return request_layout(key)[1]


def draw_offset(key, part):
    return request_layout(key)[2]


def draw_hidden_in(key, part):
    key = jax.random.fold_in(key, 3)
    columns = jnp.arange(MODEL_DIM, dtype=jnp.float32) / MODEL_DIM
    rising = jnp.exp(columns * math.log(3.0))
    return (jax.random.normal(jax.random.fold_in(key, 1), (ROWS, MODEL_DIM), jnp.float32) * rising).astype(jnp.bfloat16)


def draw_cached_key_slots(key, part):
    key = jax.random.fold_in(key, 5)
    slot_count = ROWS * SLOT_CAPACITY
    base_slot = jax.random.normal(jax.random.fold_in(key, 1), (slot_count, KEY_VALUE_HEADS * HEAD_DIM), jnp.float32) * 4.0
    return base_slot.astype(jnp.bfloat16)


def levels(key, extent, shards, least, top_value):
    level, own = 1.0, jax.random.fold_in(key, 6)
    for axis_at, parts in shards:
        heights = jnp.exp(jax.random.uniform(jax.random.fold_in(own, axis_at), (parts,), jnp.float32, least / len(shards), top_value / len(shards)))
        level = level * jnp.repeat(heights, extent[axis_at] // parts).reshape([-1 if axis == axis_at else 1 for axis in range(len(extent))])
    return level


def scatter_about(rng, shape, deviation, most, pieces=(), kind=jnp.bfloat16):
    array = jax.random.normal(rng, shape, jnp.float32) * deviation
    if len(pieces) > 0:
        array = levels(rng, shape, pieces, -0.22, 0.18) * array
    return jnp.clip(array, min=-most, max=most).astype(kind)


def setup_inputs(seed: int = 0, part: int = 0) -> dict:
    key_list = jax.random.split(jax.random.key(seed), 15)
    own_keys = jax.random.split(jax.random.fold_in(key_list[14], part), 15)
    hidden_in = draw_hidden_in(jax.random.fold_in(jax.random.fold_in(key_list[14], part), 71), part)
    attn_gain = jnp.clip(1.0 + 0.1 * jax.random.normal(key_list[1], (MODEL_DIM,), jnp.float32), 0.5, 1.5).astype(jnp.bfloat16)
    w_query = scatter_about(key_list[2], (MODEL_DIM, QUERY_HEADS * HEAD_DIM), MODEL_DIM ** -0.5, 0.0625, ((0, 64),))
    key_value_weight = scatter_about(key_list[3], (MODEL_DIM, 2 * KEY_VALUE_HEADS * HEAD_DIM), (MODEL_DIM // 16) ** -0.5, 0.25, ((0, 64),))
    w_out = scatter_about(key_list[4], (QUERY_HEADS * HEAD_DIM, MODEL_DIM), (QUERY_HEADS * HEAD_DIM // 4) ** -0.5, 0.1875, ((1, 64),))
    ffn_gain = jnp.clip(1.0 + 0.1 * jax.random.normal(key_list[5], (MODEL_DIM,), jnp.float32), 0.5, 1.5).astype(jnp.bfloat16)
    w_gate = scatter_about(key_list[6], (MODEL_DIM, FF), MODEL_DIM ** -0.5, 0.0625, ((1, 64),))
    w_up = scatter_about(key_list[7], (MODEL_DIM, FF), MODEL_DIM ** -0.5, 0.0625, ((1, 64),))
    w_down = scatter_about(key_list[8], (FF, MODEL_DIM), (FF // 4) ** -0.5, 0.09375, ((0, 64),))
    cached_key_slots = draw_cached_key_slots(jax.random.fold_in(jax.random.fold_in(key_list[14], part), 71), part)
    cached_value_slots = scatter_about(own_keys[10], (N_POOL * SLOT_CAPACITY, KEY_VALUE_HEADS * HEAD_DIM), 1.0, 6.0, ((0, 64),))
    lengths = draw_lengths(jax.random.fold_in(jax.random.fold_in(key_list[14], part), 71), part)
    home_device = draw_home_device(jax.random.fold_in(jax.random.fold_in(key_list[14], part), 71), part)
    offset = draw_offset(jax.random.fold_in(jax.random.fold_in(key_list[14], part), 71), part)
    return {"hidden_in": hidden_in, "attn_gain": attn_gain, "w_query": w_query, "key_value_weight": key_value_weight, "w_out": w_out, "ffn_gain": ffn_gain, "w_gate": w_gate, "w_up": w_up, "w_down": w_down, "cached_key_slots": cached_key_slots, "cached_value_slots": cached_value_slots, "lengths": lengths, "home_device": home_device, "offset": offset}


EPSILON = 1e-05

def normalize(value_matrix, gain):
    floats = value_matrix.astype(jnp.float32)
    factor = lax.rsqrt(lax.optimization_barrier(jnp.mean(floats * floats, axis=1, keepdims=True)) + EPSILON)
    return (floats * factor * gain.astype(jnp.float32)).astype(jnp.bfloat16)

def attend(single_query_row, incoming_key, incoming_value, key_matrix, value_matrix, start, length):
    group_size = QUERY_HEADS // KEY_VALUE_HEADS
    query_head_rows = single_query_row.astype(jnp.float32).reshape(KEY_VALUE_HEADS, group_size, HEAD_DIM)
    key_head_rows = key_matrix.astype(jnp.float32).reshape(SLOT_CAPACITY, KEY_VALUE_HEADS, HEAD_DIM)
    value_head_rows = value_matrix.astype(jnp.float32).reshape(SLOT_CAPACITY, KEY_VALUE_HEADS, HEAD_DIM)
    current_key = incoming_key.astype(jnp.float32).reshape(KEY_VALUE_HEADS, HEAD_DIM)
    current_value = incoming_value.astype(jnp.float32).reshape(KEY_VALUE_HEADS, HEAD_DIM)
    factor = HEAD_DIM ** (-0.5)
    scores = jnp.einsum('kgd,ckd->kgc', query_head_rows, key_head_rows, precision=lax.Precision.HIGHEST) * factor
    slots = jnp.arange(SLOT_CAPACITY, dtype=jnp.int32)
    live = (slots >= start) & (slots < start + length - 1)
    scores = jnp.where(live, scores, -1e+30)
    own_score = jnp.einsum('kgd,kd->kg', query_head_rows, current_key, precision=lax.Precision.HIGHEST) * factor
    top = jnp.maximum(lax.optimization_barrier(jnp.max(scores, axis=-1)), own_score)
    weights = jnp.where(live, jnp.exp(scores - top[..., None]), 0.0)
    own_weight = jnp.exp(own_score - top)
    total = lax.optimization_barrier(jnp.sum(weights, axis=-1)) + own_weight
    rounded = lax.optimization_barrier(weights.astype(jnp.bfloat16)).astype(jnp.float32)
    own_rounded = lax.optimization_barrier(own_weight.astype(jnp.bfloat16)).astype(jnp.float32)
    mixed = jnp.einsum('kgc,ckd->kgd', rounded, value_head_rows, precision=lax.Precision.HIGHEST)
    mixed = mixed + own_rounded[..., None] * current_value[:, None, :]
    return (mixed / total[..., None]).reshape(QUERY_HEADS * HEAD_DIM).astype(jnp.bfloat16)

def reference(hidden_in, attn_gain, w_query, key_value_weight, w_out, ffn_gain, w_gate, w_up, w_down, cached_key_slots, cached_value_slots, lengths, home_device, offset):
    normed = normalize(hidden_in, attn_gain)
    queries = jnp.dot(normed, w_query, preferred_element_type=jnp.float32).astype(jnp.bfloat16)
    fresh = jnp.dot(normed, key_value_weight, preferred_element_type=jnp.float32).astype(jnp.bfloat16)
    key_value_width = KEY_VALUE_HEADS * HEAD_DIM
    new_keys = fresh[:, :key_value_width]
    new_values = fresh[:, key_value_width:]
    key_blocks = cached_key_slots.reshape(N_POOL, SLOT_CAPACITY, key_value_width)
    value_blocks = cached_value_slots.reshape(N_POOL, SLOT_CAPACITY, key_value_width)

    def per_row(item):
        single_query_row, key_row, value_row, device, start, length = item
        key_matrix = key_blocks[device]
        value_matrix = value_blocks[device]
        return attend(single_query_row, key_row, value_row, key_matrix, value_matrix, start, length)
    attended = lax.map(per_row, (queries, new_keys, new_values, home_device, offset, lengths))
    residual = (hidden_in.astype(jnp.float32) + jnp.dot(attended, w_out, preferred_element_type=jnp.float32)).astype(jnp.bfloat16)
    normed_ffn = normalize(residual, ffn_gain)
    gate = jnp.dot(normed_ffn, w_gate, preferred_element_type=jnp.float32)
    upward = jnp.dot(normed_ffn, w_up, preferred_element_type=jnp.float32)
    inner = (jax.nn.silu(gate) * upward).astype(jnp.bfloat16)
    down = jnp.dot(inner, w_down, preferred_element_type=jnp.float32)
    return (residual.astype(jnp.float32) + down).astype(jnp.bfloat16)
```

```python
import jax
import jax.numpy as jnp
from jax import lax
from jax.experimental import pallas as pl
from jax.experimental.pallas import tpu as pltpu
from jax.sharding import PartitionSpec as P

MESH = pl.DeviceIdType.MESH
F32 = jnp.float32
BF16 = jnp.bfloat16
EPSILON = 1e-05
MODEL = 8192
SLOTS = 5120
CHUNK = 512
SHIFTS = (2, 1, 3, 0)
EXTRA = 7


def dot(a, b):
    return jnp.dot(a, b, preferred_element_type=F32)


def iota(shape, axis):
    return lax.broadcasted_iota(jnp.int32, shape, axis)


def kernel(
    hidden_ref,
    gain_ref,
    ffn_gain_ref,
    lengths_ref,
    home_ref,
    offset_ref,
    wq_hbm,
    wkv_hbm,
    wout_hbm,
    wgate_hbm,
    wup_hbm,
    wdown_hbm,
    keys_hbm,
    values_hbm,
    out_ref,
    wq,
    wkv,
    wout,
    wgate,
    wup,
    wdown,
    keys,
    values,
    blk,
    ext,
    sib_out,
    sib_in,
    rs_out,
    rs_in,
    qe_buf,
    qe,
    scores,
    att_buf,
    xo_out,
    xo_in,
    xr_out,
    xr_in,
    xa_buf,
    spread,
    lhs,
    res_buf,
    lhs_ffn,
    stage,
    dsib_out,
    dsib_in,
    drs_out,
    drs_in,
    load_sem,
    sib_send,
    sib_recv,
    rs_send,
    rs_recv,
    ag_send,
    ag_recv,
    fwd_send,
    fwd_recv,
    dsib_send,
    dsib_recv,
):
    me = lax.axis_index("pool")
    chip = lax.div(me, 2)
    core = lax.rem(me, 2)
    z = lax.div(chip, 8)
    x = lax.rem(lax.div(chip, 2), 4)
    y = lax.rem(chip, 2)
    sibling = chip * 2 + (1 - core)
    my_slot = core * 32 + chip

    def target(a, k):
        b = 3 - lax.div(k, 2)
        e = 1 - lax.rem(k, 2)
        return lax.rem(z + a, 4) * 8 + lax.rem(x + b, 4) * 2 + lax.rem(y + e, 2)

    def each_chip(body):
        for a in SHIFTS:

            def step(k, carry, a=a):
                body(a, target(a, k))
                return carry

            lax.fori_loop(0, 8 if a else 7, step, 0)

    def remote(src, dst, send, recv, chip_to):
        return pltpu.make_async_remote_copy(
            src_ref=src,
            dst_ref=dst,
            send_sem=send,
            recv_sem=recv,
            device_id={"pool": chip_to * 2 + core},
            device_id_type=MESH,
        )

    def to_sibling(src, dst, send, recv):
        return pltpu.make_async_remote_copy(
            src_ref=src,
            dst_ref=dst,
            send_sem=send,
            recv_sem=recv,
            device_id={"pool": sibling},
            device_id_type=MESH,
        )

    barrier = pltpu.get_barrier_semaphore()
    each_chip(
        lambda a, c: pl.semaphore_signal(
            barrier, inc=1, device_id={"pool": c * 2 + core}, device_id_type=MESH
        )
    )
    pl.semaphore_signal(barrier, inc=1, device_id={"pool": sibling}, device_id_type=MESH)

    loads = [
        pltpu.make_async_copy(src, dst, load_sem.at[i])
        for i, (src, dst) in enumerate(
            [
                (wq_hbm, wq),
                (wkv_hbm, wkv),
                (keys_hbm, keys),
                (values_hbm, values),
                (wout_hbm, wout),
                (wgate_hbm, wgate),
                (wup_hbm, wup),
                (wdown_hbm, wdown),
            ]
        )
    ]
    for load in loads:
        load.start()

    home_row = jnp.broadcast_to(home_ref[...].astype(F32), (64, 64))
    down_i = iota((64, 64), 0)
    along_i = iota((64, 64), 1)
    eye = down_i == along_i

    def column(row):
        return jnp.sum(jnp.where(eye, row, 0.0), axis=1, keepdims=True)

    home_col = column(home_row)
    same = jnp.where(home_col == home_row, 1.0, 0.0)
    rank_row = jnp.sum(jnp.where(down_i < along_i, same, 0.0), axis=0, keepdims=True)
    rank_col = jnp.sum(jnp.where(along_i < down_i, same, 0.0), axis=1, keepdims=True)
    extra_col = jnp.where(rank_col > 0.0, 1.0, 0.0)
    extra_row = jnp.where(rank_row > 0.0, 1.0, 0.0)
    order_row = jnp.sum(jnp.where(down_i < along_i, extra_col, 0.0), axis=0, keepdims=True)
    order_col = jnp.sum(jnp.where(along_i < down_i, extra_row, 0.0), axis=1, keepdims=True)
    half_row = jnp.floor(home_row[:1] * 0.5)
    half_col = jnp.floor(home_col * 0.5)
    slot_row = jnp.where(
        rank_row == 0.0, (home_row[:1] - 2.0 * half_row) * 32.0 + half_row, 64.0 + order_row
    )
    slot_col = jnp.where(
        rank_col == 0.0, (home_col - 2.0 * half_col) * 32.0 + half_col, 64.0 + order_col
    )
    to_slots = jnp.where(slot_row == iota((72, 64), 0).astype(F32), 1.0, 0.0).astype(BF16)
    from_slots = jnp.where(slot_col == iota((64, 72), 1).astype(F32), 1.0, 0.0).astype(BF16)
    here_row = home_row[:1] == me.astype(F32)
    here_col = home_col == me.astype(F32)
    lane = iota((1, 128), 1)
    lane_request = lax.div(lane, 32)
    offset_row = offset_ref[...].astype(F32)
    past_row = lengths_ref[...].astype(F32) - 1.0
    start = jnp.zeros((1, 128), F32)
    stop = jnp.zeros((1, 128), F32)
    for m in range(4):
        chosen = here_row & (rank_row == float(m))
        begin = jnp.sum(jnp.where(chosen, offset_row, 0.0), axis=1, keepdims=True)
        end = begin + jnp.sum(jnp.where(chosen, past_row, 0.0), axis=1, keepdims=True)
        start = jnp.where(lane_request == m, begin, start)
        stop = jnp.where(lane_request == m, end, stop)
    start = start.astype(jnp.int32)
    stop = stop.astype(jnp.int32)
    pick_col, pick_row = [], []
    order_is = (order_row == iota((8, 64), 0).astype(F32)) & (extra_row > 0.0)
    lane64 = lax.rem(iota((64, 128), 1), 64).astype(F32)
    order_at = (order_col == lane64) & (extra_col > 0.0)
    for m in range(1, 4):
        mine = jnp.where(here_row & (rank_row == float(m)), 1.0, 0.0)
        pick_col.append(jnp.sum(jnp.where(order_is, mine, 0.0), axis=1, keepdims=True))
        mine = jnp.where(here_col & (rank_col == float(m)), 1.0, 0.0)
        pick_row.append(jnp.sum(jnp.where(order_at, mine, 0.0), axis=0, keepdims=True))

    rows = dot(to_slots, hidden_ref[...])
    squares = jnp.sum(rows * rows, axis=1, keepdims=True)
    scaled = (rows * gain_ref[...].astype(F32)).astype(BF16)
    loads[0].wait()
    loads[1].wait()
    for n in range(10):
        weight = wq[:, n * 512 : (n + 1) * 512] if n < 8 else wkv[:, (n - 8) * 512 : (n - 7) * 512]
        part = dot(scaled, weight)
        for t in range(4):
            j = 4 * n + t
            tile = part[:, t * 128 : (t + 1) * 128]
            blk[pl.ds(j, 64, stride=48), :] = tile[:64]
            ext[pl.ds(j, 8, stride=40), :] = tile[64:]
    for e in range(8):
        for r in range(5):
            blk[pl.ds(8 * e * 48 + 40 + r, 8, stride=48), :] = ext[pl.ds(e * 40 + r * 8, 8), :]

    def high_low(value, low):
        high = value.astype(BF16).astype(F32)
        return jnp.where(low, value - high, high)

    wide = jnp.broadcast_to(squares, (72, 128))
    blk[pl.ds(45, 64, stride=48), :] = high_low(wide[:64], iota((64, 128), 1) >= 64)
    extra_squares = jnp.where(lax.rem(iota((8, 128), 1), 64) == iota((8, 128), 0), wide[64:], 0.0)
    extra_squares = jnp.sum(extra_squares, axis=0, keepdims=True)
    blk[pl.ds(46, 64, stride=48), :] = jnp.broadcast_to(
        high_low(extra_squares, lane >= 64), (64, 128)
    )
    blk[pl.ds(47, 64, stride=48), :] = jnp.zeros((64, 128), F32)

    def block(slot):
        return blk[pl.ds(pl.multiple_of(slot * 48, 16), 48), :]

    def pack_sibling(k, carry):
        sib_out[k] = block((1 - core) * 32 + k).astype(BF16)
        return carry

    lax.fori_loop(0, 32, pack_sibling, 0)
    pl.semaphore_wait(barrier, 32)
    exchange = to_sibling(sib_out, sib_in, sib_send.at[0], sib_recv.at[0])
    exchange.start()
    exchange.wait()

    def pack(k, carry):
        rs_out[k] = (block(core * 32 + k) + sib_in[k].astype(F32)).astype(BF16)
        return carry

    lax.fori_loop(0, 32, pack, 0)
    each_chip(
        lambda a, c: remote(rs_out.at[c], rs_in.at[chip], rs_send.at[0], rs_recv.at[0], c).start()
    )
    rs_in[chip] = rs_out[chip]
    part31 = pl.ds(0, 31)
    done = remote(rs_out.at[part31], rs_in.at[part31], rs_send.at[0], rs_recv.at[0], chip)
    done.wait_recv()

    def add(k, total):
        return total + rs_in[k].astype(F32)

    summed = lax.fori_loop(0, 32, add, jnp.zeros((48, 128), F32))
    done.wait_send()

    def gather_start(buf, p):
        each_chip(
            lambda a, c: remote(
                buf.at[my_slot], buf.at[my_slot], ag_send.at[p], ag_recv.at[p * 4 + a], c
            ).start()
        )

    def gather_forward(buf, p):
        sends = []
        for a in SHIFTS:
            some = buf.at[pl.ds(0, 8 if a else 7)]
            remote(some, some, ag_send.at[p], ag_recv.at[p * 4 + a], chip).wait_recv()
            group = buf.at[pl.ds(core * 32 + lax.rem(z + 4 - a, 4) * 8, 8)]
            send = to_sibling(group, group, fwd_send.at[p * 4 + a], fwd_recv.at[p * 4 + a])
            send.start()
            sends.append(send)
        return sends

    def gather_end(buf, p, sends):
        for send in sends:
            send.wait()
        some = buf.at[pl.ds(0, 31)]
        remote(some, some, ag_send.at[p], ag_recv.at[p * 4], chip).wait_send()

    qe_buf[my_slot] = summed[40:48]
    gather_start(qe_buf, 0)
    sends = gather_forward(qe_buf, 0)
    gather_end(qe_buf, 0, sends)

    own_squares = jnp.sum(summed[45:46], axis=1, keepdims=True) * (1.0 / 64.0)
    requests = [summed[:40] * lax.rsqrt(own_squares * (1.0 / MODEL) + EPSILON)]
    for e in range(EXTRA):
        for r in range(5):
            piece = qe_buf[pl.ds(8 * e, 8), r, :]
            qe[e, pl.ds(8 * r, 8), :] = piece
    for m in range(3):
        total = jnp.zeros((40, 128), F32)
        for e in range(EXTRA):
            total = total + pick_col[m][e : e + 1] * qe[e]
        sq = jnp.sum(pick_row[m] * summed[46:47], axis=1, keepdims=True)
        requests.append(total * lax.rsqrt(sq * (1.0 / MODEL) + EPSILON))
    query = jnp.concatenate([r[:32] for r in requests], axis=0).astype(BF16).astype(F32)
    new_keys = jnp.concatenate([r[32:36] for r in requests], axis=0).astype(BF16)
    new_values = jnp.concatenate([r[36:40] for r in requests], axis=0).astype(BF16)
    query_t = query.T
    lane_head = lax.rem(lax.div(iota((128, 128), 1), 8), 4)
    spread_query = jnp.concatenate(
        [jnp.where(lane_head == k, query_t, 0.0) for k in range(4)], axis=0
    ).astype(BF16)
    scale = 128.0**-0.5
    own = dot(new_keys, query_t.astype(BF16)) * scale
    own = jnp.sum(
        jnp.where(lax.div(iota((16, 128), 1), 8) == iota((16, 128), 0), own, 0.0),
        axis=0,
        keepdims=True,
    )

    loads[2].wait()

    def score(i, best):
        at = pl.ds(pl.multiple_of(i * CHUNK, CHUNK), CHUNK)
        s = dot(keys[at, :], spread_query) * scale
        slot = iota((CHUNK, 128), 0) + i * CHUNK
        s = jnp.where((slot >= start) & (slot < stop), s, -jnp.inf)
        scores[at, :] = s
        return jnp.maximum(best, jnp.max(s.reshape(CHUNK // 8, 8, 128), axis=0))

    best = lax.fori_loop(0, SLOTS // CHUNK, score, jnp.full((8, 128), -jnp.inf, F32))
    top = jnp.maximum(jnp.max(best, axis=0, keepdims=True), own)
    loads[3].wait()

    def mix(i, carry):
        total, mixed = carry
        at = pl.ds(pl.multiple_of(i * CHUNK, CHUNK), CHUNK)
        w = jnp.exp(scores[at, :] - top)
        total = total + jnp.sum(w.reshape(CHUNK // 8, 8, 128), axis=0)
        mixed = mixed + lax.dot_general(
            w.astype(BF16), values[at, :], (((0,), (0,)), ((), ())), preferred_element_type=F32
        )
        return total, mixed

    total, mixed = lax.fori_loop(
        0, SLOTS // CHUNK, mix, (jnp.zeros((8, 128), F32), jnp.zeros((128, 512), F32))
    )
    own_weight = jnp.exp(own - top)
    total = jnp.sum(total, axis=0, keepdims=True) + own_weight
    eye128 = iota((128, 128), 0) == iota((128, 128), 1)
    total_col = jnp.sum(jnp.where(eye128, total, 0.0), axis=1, keepdims=True)
    own_col = jnp.sum(jnp.where(eye128, own_weight, 0.0), axis=1, keepdims=True)
    row_head = lax.rem(lax.div(iota((128, 128), 0), 8), 4)
    att = jnp.zeros((128, 128), F32)
    for k in range(4):
        att = jnp.where(row_head == k, mixed[:, k * 128 : (k + 1) * 128], att)
    own_spread = jnp.where(lax.div(iota((128, 16), 0), 8) == iota((128, 16), 1), own_col, 0.0)
    att = (att + dot(own_spread.astype(BF16), new_values)) / total_col

    att_buf[my_slot] = att[:32].astype(BF16)
    gather_start(att_buf, 1)
    for e in range(EXTRA):
        piece = jnp.zeros((32, 128), F32)
        for m in range(3):
            piece = piece + pick_col[m][e : e + 1] * att[32 * (m + 1) : 32 * (m + 2)]
        xo_out[2 * e] = piece[:16].astype(BF16)
        xo_out[2 * e + 1] = piece[16:].astype(BF16)
    exchange = to_sibling(
        xo_out.at[pl.ds((1 - core) * 7, 7)], xo_in, sib_send.at[1], sib_recv.at[1]
    )
    exchange.start()
    exchange.wait()

    def reducer(j):
        return 5 * j + core

    def reduce_send(j, carry):
        xr_out[j] = (xo_out[core * 7 + j].astype(F32) + xo_in[j].astype(F32)).astype(BF16)

        @pl.when(reducer(j) == chip)
        def _():
            xr_in[chip] = xr_out[j]

        @pl.when(reducer(j) != chip)
        def _():
            remote(
                xr_out.at[j], xr_in.at[chip], rs_send.at[1], rs_recv.at[1], reducer(j)
            ).start()

        return carry

    lax.fori_loop(0, 7, reduce_send, 0)
    is_reducer = lax.rem(chip + 5 - core, 5) == 0
    my_chunk = lax.div(chip - core, 5)

    def many(ref, n, send, recv):
        some = ref.at[pl.ds(0, n)]
        return remote(some, some, send, recv, chip)

    @pl.when(is_reducer)
    def _():
        many(xr_in, 31, rs_send.at[1], rs_recv.at[1]).wait_recv()
        xa_buf[core * 7 + my_chunk] = lax.fori_loop(
            0, 32, lambda k, t: t + xr_in[k].astype(F32), jnp.zeros((16, 128), F32)
        ).astype(BF16)
        mine = xa_buf.at[core * 7 + my_chunk]
        each_chip(lambda a, c: remote(mine, mine, rs_send.at[2], rs_recv.at[2], c).start())
        many(xr_out, 6, rs_send.at[1], rs_recv.at[1]).wait_send()
        many(xa_buf, 6, rs_send.at[2], rs_recv.at[2]).wait_recv()

    @pl.when(jnp.logical_not(is_reducer))
    def _():
        many(xr_out, 7, rs_send.at[1], rs_recv.at[1]).wait_send()
        many(xa_buf, 7, rs_send.at[2], rs_recv.at[2]).wait_recv()

    half = xa_buf.at[pl.ds(core * 7, 7)]
    exchange = to_sibling(half, half, sib_send.at[2], sib_recv.at[2])
    exchange.start()
    sends = gather_forward(att_buf, 1)
    gather_end(att_buf, 1, sends)
    exchange.wait()

    @pl.when(is_reducer)
    def _():
        many(xr_in, 31, rs_send.at[2], rs_recv.at[2]).wait_send()

    def widen(s, carry):
        spread[pl.ds(pl.multiple_of(s * 32, 32), 32), :] = att_buf[s].astype(F32)
        return carry

    lax.fori_loop(0, 64, widen, 0)
    for q in range(14):
        spread[pl.ds(2048 + 16 * q, 16), :] = xa_buf[q].astype(F32)
    spread[pl.ds(2048 + 224, 32), :] = jnp.zeros((32, 128), F32)
    for h in range(32):
        lhs[:, h * 128 : (h + 1) * 128] = spread[pl.ds(h, 72, stride=32), :].astype(BF16)
    loads[4].wait()
    projected = dot(lhs[...], wout[...])
    moved = jnp.zeros((64, 128), F32)
    for _ in range(3):
        piece = projected.astype(BF16)
        moved = moved + dot(from_slots, piece)
        projected = projected - piece.astype(F32)
    residual = (hidden_ref[...].astype(F32) + moved).astype(BF16)

    res_buf[my_slot] = residual
    gather_start(res_buf, 2)
    sends = gather_forward(res_buf, 2)
    gather_end(res_buf, 2, sends)

    def scale_ffn(p, squares):
        value = res_buf[lax.rem(p, 2) * 32 + lax.div(p, 2)].astype(F32)
        gain = ffn_gain_ref[pl.ds(p, 1), :]
        lhs_ffn[:, pl.ds(pl.multiple_of(p * 128, 128), 128)] = (value * gain).astype(BF16)
        return squares + value * value

    squares = lax.fori_loop(0, 64, scale_ffn, jnp.zeros((64, 128), F32))
    factor = lax.rsqrt(jnp.sum(squares, axis=1, keepdims=True) * (1.0 / MODEL) + EPSILON)
    loads[5].wait()
    loads[6].wait()

    def hidden_units(i, carry):
        gate, up = carry
        at = pl.ds(pl.multiple_of(i * 1024, 1024), 1024)
        some = lhs_ffn[:, at]
        return gate + dot(some, wgate[at, :]), up + dot(some, wup[at, :])

    zero = jnp.zeros((64, 256), F32)
    gate, up = lax.fori_loop(0, 8, hidden_units, (zero, zero))
    gate = gate * factor
    inner = (gate / (1.0 + jnp.exp(-gate)) * (up * factor)).astype(BF16)

    loads[7].wait()
    exchanges = []
    for i, a in enumerate(SHIFTS):
        first = lax.rem(z + a, 4)
        for n in range(4):
            at = pl.multiple_of(first * 2048 + n * 512, 512)
            part = dot(inner, wdown[:, pl.ds(at, 512)])
            for t in range(4):
                stage[16 * i + 4 * n + t] = part[:, t * 128 : (t + 1) * 128]

        def pack_down(k, carry, i=i):
            dsib_out[8 * i + k] = stage[16 * i + 2 * k + 1 - core].astype(BF16)
            return carry

        lax.fori_loop(0, 8, pack_down, 0)
        group = pl.ds(8 * i, 8)
        exchange = to_sibling(
            dsib_out.at[group], dsib_in.at[group], dsib_send.at[i], dsib_recv.at[i]
        )
        exchange.start()
        exchanges.append(exchange)
    for i, a in enumerate(SHIFTS):
        exchanges[i].wait_recv()
        first = lax.rem(z + a, 4) * 8

        def send_down(k, carry, a=a, i=i, first=first):
            c = target(a, k)
            n = 8 * i + c - first
            total = stage[16 * i + 2 * (c - first) + core] + dsib_in[n].astype(F32)
            drs_out[n] = total.astype(BF16)
            remote(drs_out.at[n], drs_in.at[chip], rs_send.at[3], rs_recv.at[3], c).start()
            return carry

        lax.fori_loop(0, 8 if a else 7, send_down, 0)
    k = chip - z * 8
    drs_in[chip] = (stage[48 + 2 * k + core] + dsib_in[24 + k].astype(F32)).astype(BF16)
    done = many(drs_in, 31, rs_send.at[3], rs_recv.at[3])
    done.wait_recv()
    shares = lax.fori_loop(
        0, 32, lambda k, t: t + drs_in[k].astype(F32), jnp.zeros((64, 128), F32)
    )
    out_ref[...] = (residual.astype(F32) + shares).astype(BF16)
    done.wait_send()
    for exchange in exchanges:
        exchange.wait_send()


def local(
    hidden_in,
    attn_gain,
    w_query,
    key_value_weight,
    w_out,
    ffn_gain,
    w_gate,
    w_up,
    w_down,
    cached_key_slots,
    cached_value_slots,
    lengths,
    home_device,
    offset,
):
    vmem = pl.BlockSpec(memory_space=pltpu.VMEM)
    hbm = pl.BlockSpec(memory_space=pl.ANY)
    V = pltpu.VMEM
    dma = pltpu.SemaphoreType.DMA
    return pl.pallas_call(
        kernel,
        out_shape=jax.ShapeDtypeStruct((64, 128), BF16),
        in_specs=[vmem] * 6 + [hbm] * 8,
        out_specs=vmem,
        scratch_shapes=[
            V((128, 4096), BF16),
            V((128, 1024), BF16),
            V((4096, 128), BF16),
            V((8192, 256), BF16),
            V((8192, 256), BF16),
            V((256, 8192), BF16),
            V((SLOTS, 512), BF16),
            V((SLOTS, 512), BF16),
            V((64 * 48, 128), F32),
            V((320, 128), F32),
            V((32, 48, 128), BF16),
            V((32, 48, 128), BF16),
            V((32, 48, 128), BF16),
            V((32, 48, 128), BF16),
            V((64, 8, 128), F32),
            V((7, 40, 128), F32),
            V((SLOTS, 128), F32),
            V((64, 32, 128), BF16),
            V((14, 16, 128), BF16),
            V((7, 16, 128), BF16),
            V((7, 16, 128), BF16),
            V((32, 16, 128), BF16),
            V((14, 16, 128), BF16),
            V((72 * 32, 128), F32),
            V((72, 4096), BF16),
            V((64, 64, 128), BF16),
            V((64, 8192), BF16),
            V((64, 64, 128), F32),
            V((32, 64, 128), BF16),
            V((32, 64, 128), BF16),
            V((32, 64, 128), BF16),
            V((32, 64, 128), BF16),
            dma((8,)),
            dma((3,)),
            dma((3,)),
            dma((4,)),
            dma((4,)),
            dma((3,)),
            dma((12,)),
            dma((12,)),
            dma((12,)),
            dma((4,)),
            dma((4,)),
        ],
        compiler_params=pltpu.CompilerParams(
            collective_id=0, has_side_effects=True, vmem_limit_bytes=60 << 20
        ),
    )(
        hidden_in,
        attn_gain.reshape(1, 128),
        ffn_gain.reshape(64, 128).astype(F32),
        lengths.reshape(1, 64),
        home_device.reshape(1, 64),
        offset.reshape(1, 64),
        w_query,
        key_value_weight,
        w_out,
        w_gate,
        w_up,
        w_down,
        cached_key_slots,
        cached_value_slots,
    )


def solution(mesh):
    return jax.shard_map(
        local,
        mesh=mesh,
        in_specs=(
            P("unit", "pool"),
            P("pool"),
            P("pool", None),
            P("pool", None),
            P(None, "pool"),
            P(),
            P(None, "pool"),
            P(None, "pool"),
            P("pool", None),
            P(("unit", "pool"), None),
            P(("unit", "pool"), None),
            P("unit"),
            P("unit"),
            P("unit"),
        ),
        out_specs=P("unit", "pool"),
        check_vma=False,
    )
```

```python
import jax
import jax.numpy as jnp
from jax import lax
from jax.experimental import pallas as pl
from jax.experimental.pallas import tpu as pltpu
from jax.sharding import PartitionSpec as P

MESH = pl.DeviceIdType.MESH
F32 = jnp.float32
BF16 = jnp.bfloat16
EPSILON = 1e-05
MODEL = 8192
SLOTS = 5120
CHUNK = 512
SHIFTS = (2, 1, 3, 0)
EXTRA = 7


def dot(a, b):
    return jnp.dot(a, b, preferred_element_type=F32)


def iota(shape, axis):
    return lax.broadcasted_iota(jnp.int32, shape, axis)


def kernel(
    hidden_ref,
    gain_ref,
    ffn_gain_ref,
    lengths_ref,
    home_ref,
    offset_ref,
    wq_hbm,
    wkv_hbm,
    wout_hbm,
    wgate_hbm,
    wup_hbm,
    wdown_hbm,
    keys_hbm,
    values_hbm,
    out_ref,
    wq,
    wkv,
    wout,
    wgate,
    wup,
    wdown,
    keys,
    values,
    blk,
    ext,
    sib_out,
    sib_in,
    rs_out,
    rs_in,
    xq_out,
    xq_in,
    xq_buf,
    scores,
    att_buf,
    xa_out,
    xa_in,
    xa_buf,
    spread,
    spread_extra,
    lhs,
    res_buf,
    stage,
    dsib_out,
    dsib_in,
    drs_out,
    drs_in,
    load_sem,
    sib_send,
    sib_recv,
    ring_send,
    ring_recv,
    rs_send,
    rs_recv,
    ag_send,
    ag_recv,
    fwd_send,
    fwd_recv,
    dsib_send,
    dsib_recv,
):
    me = lax.axis_index("pool")
    chip = lax.div(me, 2)
    core = lax.rem(me, 2)
    z = lax.div(chip, 8)
    x = lax.rem(lax.div(chip, 2), 4)
    y = lax.rem(chip, 2)
    sibling = chip * 2 + (1 - core)
    my_slot = core * 32 + chip

    def target(a, k):
        b = 3 - lax.div(k, 2)
        e = 1 - lax.rem(k, 2)
        return lax.rem(z + a, 4) * 8 + lax.rem(x + b, 4) * 2 + lax.rem(y + e, 2)

    def each_chip(body):
        for a in SHIFTS:

            def step(k, carry, a=a):
                body(a, target(a, k))
                return carry

            lax.fori_loop(0, 8 if a else 7, step, 0)

    def remote(src, dst, send, recv, chip_to):
        return pltpu.make_async_remote_copy(
            src_ref=src,
            dst_ref=dst,
            send_sem=send,
            recv_sem=recv,
            device_id={"pool": chip_to * 2 + core},
            device_id_type=MESH,
        )

    def to_sibling(src, dst, send, recv):
        return pltpu.make_async_remote_copy(
            src_ref=src,
            dst_ref=dst,
            send_sem=send,
            recv_sem=recv,
            device_id={"pool": sibling},
            device_id_type=MESH,
        )

    member = x * 2 + core

    def ring_member(i):
        g = lax.rem(member + i, 8)
        return g, (z * 8 + lax.div(g, 2) * 2 + y) * 2 + lax.rem(g, 2)

    barrier = pltpu.get_barrier_semaphore()
    each_chip(
        lambda a, c: pl.semaphore_signal(
            barrier, inc=1, device_id={"pool": c * 2 + core}, device_id_type=MESH
        )
    )
    pl.semaphore_signal(barrier, inc=1, device_id={"pool": sibling}, device_id_type=MESH)
    for i in range(1, 4):
        other = (z * 8 + lax.rem(x + i, 4) * 2 + y) * 2 + 1 - core
        pl.semaphore_signal(barrier, inc=1, device_id={"pool": other}, device_id_type=MESH)

    loads = [
        pltpu.make_async_copy(src, dst, load_sem.at[i])
        for i, (src, dst) in enumerate(
            [
                (wq_hbm, wq),
                (wkv_hbm, wkv),
                (keys_hbm, keys),
                (values_hbm, values),
                (wout_hbm, wout),
                (wgate_hbm, wgate),
                (wup_hbm, wup),
                (wdown_hbm, wdown),
            ]
        )
    ]
    loads[0].start()
    loads[1].start()

    home_row = jnp.broadcast_to(home_ref[...].astype(F32), (64, 64))
    down_i = iota((64, 64), 0)
    along_i = iota((64, 64), 1)
    eye = down_i == along_i

    def column(row):
        return jnp.sum(jnp.where(eye, row, 0.0), axis=1, keepdims=True)

    home_col = column(home_row)
    same = jnp.where(home_col == home_row, 1.0, 0.0)
    rank_row = jnp.sum(jnp.where(down_i < along_i, same, 0.0), axis=0, keepdims=True)
    rank_col = jnp.sum(jnp.where(along_i < down_i, same, 0.0), axis=1, keepdims=True)
    extra_col = jnp.where(rank_col > 0.0, 1.0, 0.0)
    extra_row = jnp.where(rank_row > 0.0, 1.0, 0.0)
    order_row = jnp.sum(jnp.where(down_i < along_i, extra_col, 0.0), axis=0, keepdims=True)
    order_col = jnp.sum(jnp.where(along_i < down_i, extra_row, 0.0), axis=1, keepdims=True)
    half_row = jnp.floor(home_row[:1] * 0.5)
    half_col = jnp.floor(home_col * 0.5)
    slot_row = jnp.where(
        rank_row == 0.0, (home_row[:1] - 2.0 * half_row) * 32.0 + half_row, 64.0 + order_row
    )
    slot_col = jnp.where(
        rank_col == 0.0, (home_col - 2.0 * half_col) * 32.0 + half_col, 64.0 + order_col
    )
    to_slots = jnp.where(slot_row == iota((72, 64), 0).astype(F32), 1.0, 0.0).astype(BF16)
    from_slots = jnp.where(slot_col == iota((64, 80), 1).astype(F32), 1.0, 0.0).astype(BF16)
    here_row = home_row[:1] == me.astype(F32)
    here_col = home_col == me.astype(F32)
    lane = iota((1, 128), 1)
    lane_request = lax.div(lane, 32)
    offset_row = offset_ref[...].astype(F32)
    past_row = lengths_ref[...].astype(F32) - 1.0
    start = jnp.zeros((1, 128), F32)
    stop = jnp.zeros((1, 128), F32)
    for m in range(4):
        chosen = here_row & (rank_row == float(m))
        begin = jnp.sum(jnp.where(chosen, offset_row, 0.0), axis=1, keepdims=True)
        end = begin + jnp.sum(jnp.where(chosen, past_row, 0.0), axis=1, keepdims=True)
        start = jnp.where(lane_request == m, begin, start)
        stop = jnp.where(lane_request == m, end, stop)
    start = start.astype(jnp.int32)
    stop = stop.astype(jnp.int32)
    def floor_div(value, n):
        return jnp.floor((value + 0.5) * (1.0 / n))

    chunk_lane = iota((1, 384), 1).astype(F32)
    chunk_of = floor_div(chunk_lane, 48)
    chunk_row = chunk_lane - 48.0 * chunk_of
    extra_of = floor_div(chunk_row, 5)
    tile_of = 5.0 * chunk_of + chunk_row - 5.0 * extra_of
    in_lane = (order_col == extra_of) & (extra_col > 0.0)
    tile_row = iota((40, 384), 0).astype(F32)
    piece_down = iota((256, 1), 0)
    piece_extra = lax.rem(lax.div(piece_down, 4), 8).astype(F32)
    piece_head = (lax.div(piece_down, 32) * 4 + lax.rem(piece_down, 4)).astype(F32)
    in_piece = (order_row == piece_extra) & (extra_row > 0.0)
    head_lane = iota((256, 32), 1).astype(F32)
    pick_query, pick_att = [], []
    for m in range(1, 4):
        mine = jnp.where(here_col & (rank_col == float(m)), 1.0, 0.0)
        along = jnp.sum(jnp.where(in_lane, mine, 0.0), axis=0, keepdims=True)
        pick_query.append(jnp.where(tile_row == tile_of, along, 0.0))
        mine = jnp.where(here_row & (rank_row == float(m)), 1.0, 0.0)
        down = jnp.sum(jnp.where(in_piece, mine, 0.0), axis=1, keepdims=True)
        pick_att.append(jnp.where(head_lane == piece_head, down, 0.0))
    pick_query = jnp.concatenate(pick_query, axis=0).astype(BF16)
    pick_att = jnp.concatenate(pick_att, axis=1).astype(BF16)

    rows = dot(to_slots, hidden_ref[...])
    squares = jnp.sum(rows * rows, axis=1, keepdims=True)
    scaled = (rows * gain_ref[...].astype(F32)).astype(BF16)
    loads[0].wait()
    loads[1].wait()
    for load in loads[2:]:
        load.start()
    for n in range(10):
        weight = wq[:, n * 512 : (n + 1) * 512] if n < 8 else wkv[:, (n - 8) * 512 : (n - 7) * 512]
        part = dot(scaled, weight)
        for t in range(4):
            j = 4 * n + t
            tile = part[:, t * 128 : (t + 1) * 128]
            blk[pl.ds(j, 64, stride=48), :] = tile[:64]
            ext[pl.ds(48 * (j // 5) + j % 5, 8, stride=5), :] = tile[64:]
    for r in range(40, 48):
        if r != 45:
            blk[pl.ds(r, 64, stride=48), :] = jnp.zeros((64, 128), F32)

    def high_low(value, low):
        high = value.astype(BF16).astype(F32)
        return jnp.where(low, value - high, high)

    wide = jnp.broadcast_to(squares, (72, 128))
    blk[pl.ds(45, 64, stride=48), :] = high_low(wide[:64], iota((64, 128), 1) >= 64)
    extra_squares = jnp.where(lax.rem(iota((8, 128), 1), 64) == iota((8, 128), 0), wide[64:], 0.0)
    extra_squares = jnp.sum(extra_squares, axis=0, keepdims=True)
    extra_squares = high_low(extra_squares, lane >= 64)
    for g in range(8):
        ext[48 * g + 40 : 48 * g + 48, :] = jnp.zeros((8, 128), F32)
        ext[48 * g + 35 : 48 * g + 36, :] = extra_squares
        xq_out[g] = ext[48 * g : 48 * g + 48, :].astype(BF16)

    def block(slot):
        return blk[pl.ds(pl.multiple_of(slot * 48, 16), 48), :]

    def pack_sibling(k, carry):
        sib_out[k] = block((1 - core) * 32 + k).astype(BF16)
        return carry

    lax.fori_loop(0, 32, pack_sibling, 0)
    pl.semaphore_wait(barrier, 35)

    def ring_start(src, dst, p):
        def step(i, carry):
            g, device = ring_member(i)
            pltpu.make_async_remote_copy(
                src_ref=src.at[g],
                dst_ref=dst.at[member],
                send_sem=ring_send.at[p],
                recv_sem=ring_recv.at[p],
                device_id={"pool": device},
                device_id_type=MESH,
            ).start()
            return carry

        lax.fori_loop(1, 8, step, 0)
        dst[member] = src[member]

    def ring_end(src, dst, p):
        part7 = pl.ds(0, 7)
        done = to_sibling(src.at[part7], dst.at[part7], ring_send.at[p], ring_recv.at[p])
        done.wait()
        total = dst[0].astype(F32)
        for g in range(1, 8):
            total = total + dst[g].astype(F32)
        return total.astype(BF16)

    ring_start(xq_out, xq_in, 0)
    exchanges = []
    for i, a in enumerate(SHIFTS):
        group = pl.ds(lax.rem(z + a, 4) * 8, 8)
        exchange = to_sibling(sib_out.at[group], sib_in.at[group], sib_send.at[i], sib_recv.at[i])
        exchange.start()
        exchanges.append(exchange)

    def pack(k):
        rs_out[k] = (block(core * 32 + k) + sib_in[k].astype(F32)).astype(BF16)

    for i, a in enumerate(SHIFTS):
        exchanges[i].wait_recv()

        def send_sum(k, carry, a=a):
            c = target(a, k)
            pack(c)
            remote(rs_out.at[c], rs_in.at[chip], rs_send.at[0], rs_recv.at[0], c).start()
            return carry

        lax.fori_loop(0, 8 if a else 7, send_sum, 0)
    pack(chip)
    rs_in[chip] = rs_out[chip]

    def gather_start(buf, p):
        each_chip(
            lambda a, c: remote(
                buf.at[my_slot], buf.at[my_slot], ag_send.at[p], ag_recv.at[p * 4 + a], c
            ).start()
        )

    def gather_forward_one(buf, p, a):
        some = buf.at[pl.ds(0, 8 if a else 7)]
        remote(some, some, ag_send.at[p], ag_recv.at[p * 4 + a], chip).wait_recv()
        group = buf.at[pl.ds(core * 32 + lax.rem(z + 4 - a, 4) * 8, 8)]
        send = to_sibling(group, group, fwd_send.at[p * 4 + a], fwd_recv.at[p * 4 + a])
        send.start()
        return send

    def gather_forward(buf, p):
        return [gather_forward_one(buf, p, a) for a in SHIFTS]

    def gather_drain(buf, p):
        some = buf.at[pl.ds(0, 31)]
        remote(some, some, ag_send.at[p], ag_recv.at[p * 4], chip).wait_send()

    def gather_end(buf, p, sends):
        for send in sends:
            send.wait()
        gather_drain(buf, p)

    xq_buf[my_slot] = ring_end(xq_out, xq_in, 0)
    gather_start(xq_buf, 0)
    sends = gather_forward(xq_buf, 0)
    part31 = pl.ds(0, 31)
    done = remote(rs_out.at[part31], rs_in.at[part31], rs_send.at[0], rs_recv.at[0], chip)
    done.wait_recv()

    def add(k, total):
        return total + rs_in[k].astype(F32)

    summed = lax.fori_loop(0, 32, add, jnp.zeros((48, 128), F32))
    done.wait_send()
    for exchange in exchanges:
        exchange.wait_send()
    gather_end(xq_buf, 0, sends)

    def ring_total(buf, g, shape):
        first = (g % 2) * 32 + (g // 2) * 2

        def step(k, total):
            return total + buf[first + k * 8].astype(F32) + buf[first + k * 8 + 1].astype(F32)

        return lax.fori_loop(0, 4, step, jnp.zeros(shape, F32))

    own_squares = jnp.sum(summed[45:46], axis=1, keepdims=True) * (1.0 / 64.0)
    first = summed[:40] * lax.rsqrt(own_squares * (1.0 / MODEL) + EPSILON)
    pieces = [ring_total(xq_buf, g, (48, 128)) for g in range(8)]
    of_extra = lax.rem(iota((48, 128), 1), 64).astype(F32) == floor_div(
        iota((48, 128), 0).astype(F32), 5
    )
    extra_factor = jnp.sum(jnp.where(of_extra, pieces[0][35:36], 0.0), axis=1, keepdims=True)
    extra_factor = lax.rsqrt(extra_factor * (1.0 / MODEL) + EPSILON)
    extra_rows = jnp.concatenate([(p * extra_factor).astype(BF16) for p in pieces], axis=0)
    further = dot(pick_query, extra_rows)
    requests = [first] + [further[40 * m : 40 * (m + 1)] for m in range(3)]
    query = jnp.concatenate([r[:32] for r in requests], axis=0).astype(BF16).astype(F32)
    new_keys = jnp.concatenate([r[32:36] for r in requests], axis=0).astype(BF16)
    new_values = jnp.concatenate([r[36:40] for r in requests], axis=0).astype(BF16)
    query_t = query.T
    lane_head = lax.rem(lax.div(iota((128, 128), 1), 8), 4)
    spread_query = jnp.concatenate(
        [jnp.where(lane_head == k, query_t, 0.0) for k in range(4)], axis=0
    ).astype(BF16)
    scale = 128.0**-0.5
    own = dot(new_keys, query_t.astype(BF16)) * scale
    own = jnp.sum(
        jnp.where(lax.div(iota((16, 128), 1), 8) == iota((16, 128), 0), own, 0.0),
        axis=0,
        keepdims=True,
    )

    loads[2].wait()

    def score(i, best):
        at = pl.ds(pl.multiple_of(i * CHUNK, CHUNK), CHUNK)
        s = dot(keys[at, :], spread_query) * scale
        slot = iota((CHUNK, 128), 0) + i * CHUNK
        s = jnp.where((slot >= start) & (slot < stop), s, -jnp.inf)
        scores[at, :] = s
        return jnp.maximum(best, jnp.max(s.reshape(CHUNK // 8, 8, 128), axis=0))

    best = lax.fori_loop(0, SLOTS // CHUNK, score, jnp.full((8, 128), -jnp.inf, F32))
    top = jnp.maximum(jnp.max(best, axis=0, keepdims=True), own)
    loads[3].wait()

    def mix(i, carry):
        total, mixed = carry
        at = pl.ds(pl.multiple_of(i * CHUNK, CHUNK), CHUNK)
        w = jnp.exp(scores[at, :] - top)
        total = total + jnp.sum(w.reshape(CHUNK // 8, 8, 128), axis=0)
        mixed = mixed + lax.dot_general(
            w.astype(BF16), values[at, :], (((0,), (0,)), ((), ())), preferred_element_type=F32
        )
        return total, mixed

    total, mixed = lax.fori_loop(
        0, SLOTS // CHUNK, mix, (jnp.zeros((8, 128), F32), jnp.zeros((128, 512), F32))
    )
    own_weight = jnp.exp(own - top)
    total = jnp.sum(total, axis=0, keepdims=True) + own_weight
    eye128 = iota((128, 128), 0) == iota((128, 128), 1)
    total_col = jnp.sum(jnp.where(eye128, total, 0.0), axis=1, keepdims=True)
    own_col = jnp.sum(jnp.where(eye128, own_weight, 0.0), axis=1, keepdims=True)
    row_head = lax.rem(lax.div(iota((128, 128), 0), 8), 4)
    att = jnp.zeros((128, 128), F32)
    for k in range(4):
        att = jnp.where(row_head == k, mixed[:, k * 128 : (k + 1) * 128], att)
    own_spread = jnp.where(lax.div(iota((128, 16), 0), 8) == iota((128, 16), 1), own_col, 0.0)
    att = (att + dot(own_spread.astype(BF16), new_values)) / total_col

    att = att.astype(BF16)
    pieces = dot(pick_att, att[32:]).astype(BF16)
    for g in range(8):
        xa_out[g] = pieces[32 * g : 32 * (g + 1)]
    ring_start(xa_out, xa_in, 1)
    att_buf[my_slot] = att[:32]
    gather_start(att_buf, 1)
    xa_buf[my_slot] = ring_end(xa_out, xa_in, 1)
    gather_start(xa_buf, 3)
    sends = gather_forward(att_buf, 1)
    extra_sends = gather_forward(xa_buf, 3)
    gather_end(att_buf, 1, sends)

    def widen(s, carry):
        spread[pl.ds(pl.multiple_of(s * 32, 32), 32), :] = att_buf[s].astype(F32)
        return carry

    lax.fori_loop(0, 64, widen, 0)
    gather_end(xa_buf, 3, extra_sends)
    for g in range(8):
        spread_extra[32 * g : 32 * (g + 1), :] = ring_total(xa_buf, g, (32, 128))
    for h in range(32):
        at = slice(h * 128, (h + 1) * 128)
        lhs[:64, at] = spread[pl.ds(h, 64, stride=32), :].astype(BF16)
        lhs[64:, at] = jnp.concatenate(
            [spread_extra[pl.ds(32 * (h // 4) + h % 4, 8, stride=4), :], jnp.zeros((8, 128), F32)],
            axis=0,
        ).astype(BF16)
    loads[4].wait()
    projected = dot(lhs[...], wout[...])
    moved = jnp.zeros((64, 128), F32)
    for _ in range(3):
        piece = projected.astype(BF16)
        moved = moved + dot(from_slots, piece)
        projected = projected - piece.astype(F32)
    residual = (hidden_ref[...].astype(F32) + moved).astype(BF16)

    res_buf[my_slot] = residual
    gather_start(res_buf, 2)
    loads[5].wait()
    loads[6].wait()

    def hidden_units(a, parity, carry):
        def step(k, carry):
            squares, gate, up = carry
            some, gates, ups = [], [], []
            for n in range(2):
                c = lax.rem(z + 4 - a, 4) * 8 + 2 * k + n
                at = pl.ds(pl.multiple_of((2 * c + parity) * 128, 128), 128)
                value = res_buf[parity * 32 + c].astype(F32)
                squares = squares + value * value
                some.append((value * ffn_gain_ref[:, at].astype(F32)).astype(BF16))
                gates.append(wgate[at, :])
                ups.append(wup[at, :])
            some = jnp.concatenate(some, axis=1)
            gate = gate + dot(some, jnp.concatenate(gates, axis=0))
            up = up + dot(some, jnp.concatenate(ups, axis=0))
            return squares, gate, up

        return lax.fori_loop(0, 4, step, carry)

    zero = jnp.zeros((64, 256), F32)
    carry = (jnp.zeros((64, 128), F32), zero, zero)
    sends = []
    for i, a in enumerate(SHIFTS):
        sends.append(gather_forward_one(res_buf, 2, a))
        carry = hidden_units(a, core, carry)
        if i:
            sends[i - 1].wait_recv()
            carry = hidden_units(SHIFTS[i - 1], 1 - core, carry)
    sends[3].wait_recv()
    squares, gate, up = hidden_units(SHIFTS[3], 1 - core, carry)
    gather_drain(res_buf, 2)
    for send in sends:
        send.wait_send()
    factor = lax.rsqrt(jnp.sum(squares, axis=1, keepdims=True) * (1.0 / MODEL) + EPSILON)
    gate = gate * factor
    inner = (gate / (1.0 + jnp.exp(-gate)) * (up * factor)).astype(BF16)

    loads[7].wait()
    exchanges = []
    for i, a in enumerate(SHIFTS):
        first = lax.rem(z + a, 4)
        for n in range(4):
            at = pl.multiple_of(first * 2048 + n * 512, 512)
            part = dot(inner, wdown[:, pl.ds(at, 512)])
            for t in range(4):
                stage[16 * i + 4 * n + t] = part[:, t * 128 : (t + 1) * 128]

        def pack_down(k, carry, i=i):
            dsib_out[8 * i + k] = stage[16 * i + 2 * k + 1 - core].astype(BF16)
            return carry

        lax.fori_loop(0, 8, pack_down, 0)
        group = pl.ds(8 * i, 8)
        exchange = to_sibling(
            dsib_out.at[group], dsib_in.at[group], dsib_send.at[i], dsib_recv.at[i]
        )
        exchange.start()
        exchanges.append(exchange)
    for i, a in enumerate(SHIFTS):
        exchanges[i].wait_recv()
        first = lax.rem(z + a, 4) * 8

        def send_down(k, carry, a=a, i=i, first=first):
            c = target(a, k)
            n = 8 * i + c - first
            total = stage[16 * i + 2 * (c - first) + core] + dsib_in[n].astype(F32)
            drs_out[n] = total.astype(BF16)
            remote(drs_out.at[n], drs_in.at[chip], rs_send.at[1], rs_recv.at[1], c).start()
            return carry

        lax.fori_loop(0, 8 if a else 7, send_down, 0)
    k = chip - z * 8
    drs_in[chip] = (stage[48 + 2 * k + core] + dsib_in[24 + k].astype(F32)).astype(BF16)
    done = remote(drs_out.at[part31], drs_in.at[part31], rs_send.at[1], rs_recv.at[1], chip)
    done.wait_recv()
    shares = lax.fori_loop(
        0, 32, lambda k, t: t + drs_in[k].astype(F32), jnp.zeros((64, 128), F32)
    )
    out_ref[...] = (residual.astype(F32) + shares).astype(BF16)
    done.wait_send()
    for exchange in exchanges:
        exchange.wait_send()


def local(
    hidden_in,
    attn_gain,
    w_query,
    key_value_weight,
    w_out,
    ffn_gain,
    w_gate,
    w_up,
    w_down,
    cached_key_slots,
    cached_value_slots,
    lengths,
    home_device,
    offset,
):
    vmem = pl.BlockSpec(memory_space=pltpu.VMEM)
    hbm = pl.BlockSpec(memory_space=pl.ANY)
    V = pltpu.VMEM
    dma = pltpu.SemaphoreType.DMA
    return pl.pallas_call(
        kernel,
        out_shape=jax.ShapeDtypeStruct((64, 128), BF16),
        in_specs=[vmem] * 6 + [hbm] * 8,
        out_specs=vmem,
        scratch_shapes=[
            V((128, 4096), BF16),
            V((128, 1024), BF16),
            V((4096, 128), BF16),
            V((8192, 256), BF16),
            V((8192, 256), BF16),
            V((256, 8192), BF16),
            V((SLOTS, 512), BF16),
            V((SLOTS, 512), BF16),
            V((64 * 48, 128), F32),
            V((8 * 48, 128), F32),
            V((32, 48, 128), BF16),
            V((32, 48, 128), BF16),
            V((32, 48, 128), BF16),
            V((32, 48, 128), BF16),
            V((8, 48, 128), BF16),
            V((8, 48, 128), BF16),
            V((64, 48, 128), BF16),
            V((SLOTS, 128), F32),
            V((64, 32, 128), BF16),
            V((8, 32, 128), BF16),
            V((8, 32, 128), BF16),
            V((64, 32, 128), BF16),
            V((64 * 32, 128), F32),
            V((256, 128), F32),
            V((80, 4096), BF16),
            V((64, 64, 128), BF16),
            V((64, 64, 128), F32),
            V((32, 64, 128), BF16),
            V((32, 64, 128), BF16),
            V((32, 64, 128), BF16),
            V((32, 64, 128), BF16),
            dma((8,)),
            dma((4,)),
            dma((4,)),
            dma((2,)),
            dma((2,)),
            dma((2,)),
            dma((2,)),
            dma((4,)),
            dma((16,)),
            dma((16,)),
            dma((16,)),
            dma((4,)),
            dma((4,)),
        ],
        compiler_params=pltpu.CompilerParams(
            collective_id=0, has_side_effects=True, vmem_limit_bytes=60 << 20
        ),
    )(
        hidden_in,
        attn_gain.reshape(1, 128),
        ffn_gain.reshape(1, 8192),
        lengths.reshape(1, 64),
        home_device.reshape(1, 64),
        offset.reshape(1, 64),
        w_query,
        key_value_weight,
        w_out,
        w_gate,
        w_up,
        w_down,
        cached_key_slots,
        cached_value_slots,
    )


def solution(mesh):
    return jax.shard_map(
        local,
        mesh=mesh,
        in_specs=(
            P("unit", "pool"),
            P("pool"),
            P("pool", None),
            P("pool", None),
            P(None, "pool"),
            P(),
            P(None, "pool"),
            P(None, "pool"),
            P("pool", None),
            P(("unit", "pool"), None),
            P(("unit", "pool"), None),
            P("unit"),
            P("unit"),
            P("unit"),
        ),
        out_specs=P("unit", "pool"),
        check_vma=False,
    )
```

```python
import jax
import jax.numpy as jnp
from jax import lax
from jax.experimental import pallas as pl
from jax.experimental.pallas import tpu as pltpu
from jax.sharding import PartitionSpec as P

MESH = pl.DeviceIdType.MESH
F32 = jnp.float32
BF16 = jnp.bfloat16
EPSILON = 1e-05
MODEL = 8192
SLOTS = 5120
SCORE = 1024
MIX = 1024
SHIFTS = (2, 1, 3, 0)
EXTRA = 7


def dot(a, b):
    return jnp.dot(a, b, preferred_element_type=F32)


def iota(shape, axis):
    return lax.broadcasted_iota(jnp.int32, shape, axis)


def kernel(
    hidden_hbm,
    gain_hbm,
    ffn_gain_hbm,
    lengths_hbm,
    home_hbm,
    offset_hbm,
    wq_hbm,
    wkv_hbm,
    wout_hbm,
    wgate_hbm,
    wup_hbm,
    wdown_hbm,
    keys_hbm,
    values_hbm,
    out_ref,
    hidden_ref,
    gain_ref,
    ffn_gain_ref,
    lengths_ref,
    home_ref,
    offset_ref,
    gain_rows,
    wq,
    wkv,
    wout,
    wgate,
    wup,
    wdown,
    keys,
    values,
    blk,
    ext,
    sib_out,
    sib_in,
    rs_out,
    rs_in,
    xq_out,
    xq_in,
    xq_buf,
    scores,
    att_buf,
    xa_out,
    xa_in,
    xa_buf,
    spread,
    spread_extra,
    lhs,
    res_buf,
    stage,
    dsib_out,
    dsib_in,
    drs_out,
    drs_in,
    load_sem,
    small_sem,
    sib_send,
    sib_recv,
    ring_send,
    ring_recv,
    rs_send,
    rs_recv,
    ag_send,
    ag_recv,
    fwd_send,
    fwd_recv,
    dsib_send,
    dsib_recv,
):
    me = lax.axis_index("pool")
    chip = lax.div(me, 2)
    core = lax.rem(me, 2)
    z = lax.div(chip, 8)
    x = lax.rem(lax.div(chip, 2), 4)
    y = lax.rem(chip, 2)
    sibling = chip * 2 + (1 - core)
    my_slot = core * 32 + chip

    def target(a, k):
        b = 3 - lax.div(k, 2)
        e = 1 - lax.rem(k, 2)
        return lax.rem(z + a, 4) * 8 + lax.rem(x + b, 4) * 2 + lax.rem(y + e, 2)

    def each_chip(body):
        for a in SHIFTS:

            def step(k, carry, a=a):
                body(a, target(a, k))
                return carry

            lax.fori_loop(0, 8 if a else 7, step, 0)

    def remote(src, dst, send, recv, chip_to):
        return pltpu.make_async_remote_copy(
            src_ref=src,
            dst_ref=dst,
            send_sem=send,
            recv_sem=recv,
            device_id={"pool": chip_to * 2 + core},
            device_id_type=MESH,
        )

    def to_sibling(src, dst, send, recv):
        return pltpu.make_async_remote_copy(
            src_ref=src,
            dst_ref=dst,
            send_sem=send,
            recv_sem=recv,
            device_id={"pool": sibling},
            device_id_type=MESH,
        )

    member = x * 2 + core

    def ring_member(i):
        g = lax.rem(member + i, 8)
        return g, (z * 8 + lax.div(g, 2) * 2 + y) * 2 + lax.rem(g, 2)

    barrier = pltpu.get_barrier_semaphore()
    each_chip(
        lambda a, c: pl.semaphore_signal(
            barrier, inc=1, device_id={"pool": c * 2 + core}, device_id_type=MESH
        )
    )
    pl.semaphore_signal(barrier, inc=1, device_id={"pool": sibling}, device_id_type=MESH)
    for i in range(1, 4):
        other = (z * 8 + lax.rem(x + i, 4) * 2 + y) * 2 + 1 - core
        pl.semaphore_signal(barrier, inc=1, device_id={"pool": other}, device_id_type=MESH)

    loads = [
        pltpu.make_async_copy(src, dst, load_sem.at[i])
        for i, (src, dst) in enumerate(
            [
                (wq_hbm, wq),
                (wkv_hbm, wkv),
                (keys_hbm, keys),
                (values_hbm, values),
                (wout_hbm, wout),
                (wgate_hbm, wgate),
                (wup_hbm, wup),
                (wdown_hbm, wdown),
            ]
        )
    ]
    small = [
        pltpu.make_async_copy(src, dst, small_sem.at[i])
        for i, (src, dst) in enumerate(
            [
                (home_hbm, home_ref),
                (hidden_hbm, hidden_ref),
                (gain_hbm, gain_ref),
                (offset_hbm, offset_ref),
                (lengths_hbm, lengths_ref),
                (ffn_gain_hbm, ffn_gain_ref),
            ]
        )
    ]
    for load in small + loads[:2]:
        load.start()
    for load in small:
        load.wait()

    gain_rows[...] = ffn_gain_ref[...].reshape(64, 128).astype(F32)

    home_row = jnp.broadcast_to(home_ref[...].astype(F32), (64, 64))
    down_i = iota((64, 64), 0)
    along_i = iota((64, 64), 1)
    eye = down_i == along_i

    def column(row):
        return jnp.sum(jnp.where(eye, row, 0.0), axis=1, keepdims=True)

    home_col = column(home_row)
    same = jnp.where(home_col == home_row, 1.0, 0.0)
    rank_row = jnp.sum(jnp.where(down_i < along_i, same, 0.0), axis=0, keepdims=True)
    rank_col = jnp.sum(jnp.where(along_i < down_i, same, 0.0), axis=1, keepdims=True)
    extra_col = jnp.where(rank_col > 0.0, 1.0, 0.0)
    extra_row = jnp.where(rank_row > 0.0, 1.0, 0.0)
    order_row = jnp.sum(jnp.where(down_i < along_i, extra_col, 0.0), axis=0, keepdims=True)
    order_col = jnp.sum(jnp.where(along_i < down_i, extra_row, 0.0), axis=1, keepdims=True)
    half_row = jnp.floor(home_row[:1] * 0.5)
    half_col = jnp.floor(home_col * 0.5)
    slot_row = jnp.where(
        rank_row == 0.0, (home_row[:1] - 2.0 * half_row) * 32.0 + half_row, 64.0 + order_row
    )
    slot_col = jnp.where(
        rank_col == 0.0, (home_col - 2.0 * half_col) * 32.0 + half_col, 64.0 + order_col
    )
    to_slots = jnp.where(slot_row == iota((72, 64), 0).astype(F32), 1.0, 0.0).astype(BF16)
    from_slots = jnp.where(slot_col == iota((64, 80), 1).astype(F32), 1.0, 0.0).astype(BF16)
    here_row = home_row[:1] == me.astype(F32)
    here_col = home_col == me.astype(F32)
    lane = iota((1, 128), 1)
    lane_request = lax.div(lane, 32)
    offset_row = offset_ref[...].astype(F32)
    past_row = lengths_ref[...].astype(F32) - 1.0
    start = jnp.zeros((1, 128), F32)
    stop = jnp.zeros((1, 128), F32)
    for m in range(4):
        chosen = here_row & (rank_row == float(m))
        begin = jnp.sum(jnp.where(chosen, offset_row, 0.0), axis=1, keepdims=True)
        end = begin + jnp.sum(jnp.where(chosen, past_row, 0.0), axis=1, keepdims=True)
        start = jnp.where(lane_request == m, begin, start)
        stop = jnp.where(lane_request == m, end, stop)
    start = start.astype(jnp.int32)
    stop = stop.astype(jnp.int32)
    def floor_div(value, n):
        return jnp.floor((value + 0.5) * (1.0 / n))

    chunk_lane = iota((1, 384), 1).astype(F32)
    chunk_of = floor_div(chunk_lane, 48)
    chunk_row = chunk_lane - 48.0 * chunk_of
    extra_of = floor_div(chunk_row, 5)
    tile_of = 5.0 * chunk_of + chunk_row - 5.0 * extra_of
    in_lane = (order_col == extra_of) & (extra_col > 0.0)
    tile_row = iota((40, 384), 0).astype(F32)
    piece_down = iota((256, 1), 0)
    piece_extra = lax.rem(lax.div(piece_down, 4), 8).astype(F32)
    piece_head = (lax.div(piece_down, 32) * 4 + lax.rem(piece_down, 4)).astype(F32)
    in_piece = (order_row == piece_extra) & (extra_row > 0.0)
    head_lane = iota((256, 32), 1).astype(F32)
    pick_query, pick_att = [], []
    for m in range(1, 4):
        mine = jnp.where(here_col & (rank_col == float(m)), 1.0, 0.0)
        along = jnp.sum(jnp.where(in_lane, mine, 0.0), axis=0, keepdims=True)
        pick_query.append(jnp.where(tile_row == tile_of, along, 0.0))
        mine = jnp.where(here_row & (rank_row == float(m)), 1.0, 0.0)
        down = jnp.sum(jnp.where(in_piece, mine, 0.0), axis=1, keepdims=True)
        pick_att.append(jnp.where(head_lane == piece_head, down, 0.0))
    pick_query = jnp.concatenate(pick_query, axis=0).astype(BF16)
    pick_att = jnp.concatenate(pick_att, axis=1).astype(BF16)

    rows = dot(to_slots, hidden_ref[...])
    squares = jnp.sum(rows * rows, axis=1, keepdims=True)
    scaled = (rows * gain_ref[...].astype(F32)).astype(BF16)
    loads[0].wait()
    loads[1].wait()
    for load in loads[2:]:
        load.start()
    for n in range(10):
        weight = wq[:, n * 512 : (n + 1) * 512] if n < 8 else wkv[:, (n - 8) * 512 : (n - 7) * 512]
        part = dot(scaled, weight)
        for t in range(4):
            j = 4 * n + t
            tile = part[:, t * 128 : (t + 1) * 128]
            blk[pl.ds(j, 64, stride=48), :] = tile[:64]
            ext[pl.ds(48 * (j // 5) + j % 5, 8, stride=5), :] = tile[64:]
    for r in range(40, 48):
        if r != 45:
            blk[pl.ds(r, 64, stride=48), :] = jnp.zeros((64, 128), F32)

    def high_low(value, low):
        high = value.astype(BF16).astype(F32)
        return jnp.where(low, value - high, high)

    wide = jnp.broadcast_to(squares, (72, 128))
    blk[pl.ds(45, 64, stride=48), :] = high_low(wide[:64], iota((64, 128), 1) >= 64)
    extra_squares = jnp.where(lax.rem(iota((8, 128), 1), 64) == iota((8, 128), 0), wide[64:], 0.0)
    extra_squares = jnp.sum(extra_squares, axis=0, keepdims=True)
    extra_squares = high_low(extra_squares, lane >= 64)
    for g in range(8):
        ext[48 * g + 40 : 48 * g + 48, :] = jnp.zeros((8, 128), F32)
        ext[48 * g + 35 : 48 * g + 36, :] = extra_squares
        xq_out[g] = ext[48 * g : 48 * g + 48, :].astype(BF16)

    def block(slot):
        return blk[pl.ds(pl.multiple_of(slot * 48, 16), 48), :]

    def pack_sibling(k, carry):
        sib_out[k] = block((1 - core) * 32 + k).astype(BF16)
        return carry

    lax.fori_loop(0, 32, pack_sibling, 0)
    pl.semaphore_wait(barrier, 35)

    def ring_start(src, dst, p):
        def step(i, carry):
            g, device = ring_member(i)
            pltpu.make_async_remote_copy(
                src_ref=src.at[g],
                dst_ref=dst.at[member],
                send_sem=ring_send.at[p],
                recv_sem=ring_recv.at[p],
                device_id={"pool": device},
                device_id_type=MESH,
            ).start()
            return carry

        lax.fori_loop(1, 8, step, 0)
        dst[member] = src[member]

    def ring_end(src, dst, p):
        part7 = pl.ds(0, 7)
        done = to_sibling(src.at[part7], dst.at[part7], ring_send.at[p], ring_recv.at[p])
        done.wait()
        total = dst[0].astype(F32)
        for g in range(1, 8):
            total = total + dst[g].astype(F32)
        return total.astype(BF16)

    ring_start(xq_out, xq_in, 0)
    exchanges = []
    for i, a in enumerate(SHIFTS):
        group = pl.ds(lax.rem(z + a, 4) * 8, 8)
        exchange = to_sibling(sib_out.at[group], sib_in.at[group], sib_send.at[i], sib_recv.at[i])
        exchange.start()
        exchanges.append(exchange)

    def pack(k):
        rs_out[k] = (block(core * 32 + k) + sib_in[k].astype(F32)).astype(BF16)

    for i, a in enumerate(SHIFTS):
        exchanges[i].wait_recv()

        def send_sum(k, carry, a=a):
            c = target(a, k)
            pack(c)
            remote(rs_out.at[c], rs_in.at[chip], rs_send.at[0], rs_recv.at[0], c).start()
            return carry

        lax.fori_loop(0, 8 if a else 7, send_sum, 0)
    pack(chip)
    rs_in[chip] = rs_out[chip]

    def gather_start(buf, p):
        each_chip(
            lambda a, c: remote(
                buf.at[my_slot], buf.at[my_slot], ag_send.at[p], ag_recv.at[p * 4 + a], c
            ).start()
        )

    def gather_forward_one(buf, p, a):
        some = buf.at[pl.ds(0, 8 if a else 7)]
        remote(some, some, ag_send.at[p], ag_recv.at[p * 4 + a], chip).wait_recv()
        group = buf.at[pl.ds(core * 32 + lax.rem(z + 4 - a, 4) * 8, 8)]
        send = to_sibling(group, group, fwd_send.at[p * 4 + a], fwd_recv.at[p * 4 + a])
        send.start()
        return send

    def gather_forward(buf, p):
        return [gather_forward_one(buf, p, a) for a in SHIFTS]

    def gather_drain(buf, p):
        some = buf.at[pl.ds(0, 31)]
        remote(some, some, ag_send.at[p], ag_recv.at[p * 4], chip).wait_send()

    def gather_end(buf, p, sends):
        for send in sends:
            send.wait()
        gather_drain(buf, p)

    xq_buf[my_slot] = ring_end(xq_out, xq_in, 0)
    gather_start(xq_buf, 0)
    sends = gather_forward(xq_buf, 0)
    part31 = pl.ds(0, 31)
    done = remote(rs_out.at[part31], rs_in.at[part31], rs_send.at[0], rs_recv.at[0], chip)
    done.wait_recv()

    def add(k, total):
        return total + rs_in[k].astype(F32)

    summed = lax.fori_loop(0, 32, add, jnp.zeros((48, 128), F32))
    done.wait_send()
    for exchange in exchanges:
        exchange.wait_send()
    gather_end(xq_buf, 0, sends)

    def ring_total(buf, g, shape):
        first = (g % 2) * 32 + (g // 2) * 2

        def step(k, total):
            return total + buf[first + k * 8].astype(F32) + buf[first + k * 8 + 1].astype(F32)

        return lax.fori_loop(0, 4, step, jnp.zeros(shape, F32))

    own_squares = jnp.sum(summed[45:46], axis=1, keepdims=True) * (1.0 / 64.0)
    first = summed[:40] * lax.rsqrt(own_squares * (1.0 / MODEL) + EPSILON)
    pieces = [ring_total(xq_buf, g, (48, 128)) for g in range(8)]
    of_extra = lax.rem(iota((48, 128), 1), 64).astype(F32) == floor_div(
        iota((48, 128), 0).astype(F32), 5
    )
    extra_factor = jnp.sum(jnp.where(of_extra, pieces[0][35:36], 0.0), axis=1, keepdims=True)
    extra_factor = lax.rsqrt(extra_factor * (1.0 / MODEL) + EPSILON)
    extra_rows = jnp.concatenate([(p * extra_factor).astype(BF16) for p in pieces], axis=0)
    further = dot(pick_query, extra_rows)
    requests = [first] + [further[40 * m : 40 * (m + 1)] for m in range(3)]
    query = jnp.concatenate([r[:32] for r in requests], axis=0).astype(BF16).astype(F32)
    new_keys = jnp.concatenate([r[32:36] for r in requests], axis=0).astype(BF16)
    new_values = jnp.concatenate([r[36:40] for r in requests], axis=0).astype(BF16)
    query_t = query.T
    lane_head = lax.rem(lax.div(iota((128, 128), 1), 8), 4)
    spread_query = jnp.concatenate(
        [jnp.where(lane_head == k, query_t, 0.0) for k in range(4)], axis=0
    ).astype(BF16)
    scale = 128.0**-0.5
    own = dot(new_keys, query_t.astype(BF16)) * scale
    own = jnp.sum(
        jnp.where(lax.div(iota((16, 128), 1), 8) == iota((16, 128), 0), own, 0.0),
        axis=0,
        keepdims=True,
    )

    loads[2].wait()

    def score(i, best):
        at = pl.ds(pl.multiple_of(i * SCORE, SCORE), SCORE)
        s = dot(keys[at, :], spread_query) * scale
        slot = iota((SCORE, 128), 0) + i * SCORE
        s = jnp.where((slot >= start) & (slot < stop), s, -jnp.inf)
        scores[at, :] = s
        return jnp.maximum(best, jnp.max(s.reshape(SCORE // 8, 8, 128), axis=0))

    best = lax.fori_loop(0, SLOTS // SCORE, score, jnp.full((8, 128), -jnp.inf, F32), unroll=True)
    top = jnp.maximum(jnp.max(best, axis=0, keepdims=True), own)
    loads[3].wait()

    def mix(i, carry):
        total, mixed = carry
        at = pl.ds(pl.multiple_of(i * MIX, MIX), MIX)
        w = jnp.exp(scores[at, :] - top)
        total = total + jnp.sum(w.reshape(MIX // 8, 8, 128), axis=0)
        mixed = mixed + lax.dot_general(
            w.astype(BF16), values[at, :], (((0,), (0,)), ((), ())), preferred_element_type=F32
        )
        return total, mixed

    total, mixed = lax.fori_loop(
        0,
        SLOTS // MIX,
        mix,
        (jnp.zeros((8, 128), F32), jnp.zeros((128, 512), F32)),
        unroll=True,
    )
    own_weight = jnp.exp(own - top)
    total = jnp.sum(total, axis=0, keepdims=True) + own_weight
    eye128 = iota((128, 128), 0) == iota((128, 128), 1)
    total_col = jnp.sum(jnp.where(eye128, total, 0.0), axis=1, keepdims=True)
    own_col = jnp.sum(jnp.where(eye128, own_weight, 0.0), axis=1, keepdims=True)
    row_head = lax.rem(lax.div(iota((128, 128), 0), 8), 4)
    att = jnp.zeros((128, 128), F32)
    for k in range(4):
        att = jnp.where(row_head == k, mixed[:, k * 128 : (k + 1) * 128], att)
    own_spread = jnp.where(lax.div(iota((128, 16), 0), 8) == iota((128, 16), 1), own_col, 0.0)
    att = (att + dot(own_spread.astype(BF16), new_values)) / total_col

    att = att.astype(BF16)
    pieces = dot(pick_att, att[32:]).astype(BF16)
    for g in range(8):
        xa_out[g] = pieces[32 * g : 32 * (g + 1)]
    ring_start(xa_out, xa_in, 1)
    att_buf[my_slot] = att[:32]
    gather_start(att_buf, 1)
    xa_buf[my_slot] = ring_end(xa_out, xa_in, 1)
    gather_start(xa_buf, 3)
    sends = gather_forward(att_buf, 1)
    extra_sends = gather_forward(xa_buf, 3)
    gather_end(att_buf, 1, sends)

    def widen(s, carry):
        spread[pl.ds(pl.multiple_of(s * 32, 32), 32), :] = att_buf[s].astype(F32)
        return carry

    lax.fori_loop(0, 64, widen, 0)
    gather_end(xa_buf, 3, extra_sends)
    for g in range(8):
        spread_extra[32 * g : 32 * (g + 1), :] = ring_total(xa_buf, g, (32, 128))
    for h in range(32):
        at = slice(h * 128, (h + 1) * 128)
        lhs[:64, at] = spread[pl.ds(h, 64, stride=32), :].astype(BF16)
        lhs[64:, at] = jnp.concatenate(
            [spread_extra[pl.ds(32 * (h // 4) + h % 4, 8, stride=4), :], jnp.zeros((8, 128), F32)],
            axis=0,
        ).astype(BF16)
    loads[4].wait()
    projected = dot(lhs[...], wout[...])
    moved = jnp.zeros((64, 128), F32)
    for _ in range(3):
        piece = projected.astype(BF16)
        moved = moved + dot(from_slots, piece)
        projected = projected - piece.astype(F32)
    residual = (hidden_ref[...].astype(F32) + moved).astype(BF16)

    res_buf[my_slot] = residual
    gather_start(res_buf, 2)
    loads[5].wait()
    loads[6].wait()

    def hidden_units(a, parity, carry):
        def step(k, carry):
            squares, gate, up = carry
            some, gates, ups = [], [], []
            for n in range(2):
                c = lax.rem(z + 4 - a, 4) * 8 + 2 * k + n
                at = pl.ds(pl.multiple_of((2 * c + parity) * 128, 128), 128)
                value = res_buf[parity * 32 + c].astype(F32)
                squares = squares + value * value
                some.append((value * gain_rows[pl.ds(2 * c + parity, 1), :]).astype(BF16))
                gates.append(wgate[at, :])
                ups.append(wup[at, :])
            some = jnp.concatenate(some, axis=1)
            gate = gate + dot(some, jnp.concatenate(gates, axis=0))
            up = up + dot(some, jnp.concatenate(ups, axis=0))
            return squares, gate, up

        return lax.fori_loop(0, 4, step, carry, unroll=True)

    zero = jnp.zeros((64, 256), F32)
    carry = (jnp.zeros((64, 128), F32), zero, zero)
    sends = []
    for i, a in enumerate(SHIFTS):
        sends.append(gather_forward_one(res_buf, 2, a))
        carry = hidden_units(a, core, carry)
        if i:
            sends[i - 1].wait_recv()
            carry = hidden_units(SHIFTS[i - 1], 1 - core, carry)
    sends[3].wait_recv()
    squares, gate, up = hidden_units(SHIFTS[3], 1 - core, carry)
    gather_drain(res_buf, 2)
    for send in sends:
        send.wait_send()
    factor = lax.rsqrt(jnp.sum(squares, axis=1, keepdims=True) * (1.0 / MODEL) + EPSILON)
    gate = gate * factor
    inner = (gate / (1.0 + jnp.exp(-gate)) * (up * factor)).astype(BF16)

    loads[7].wait()
    exchanges = []
    for i, a in enumerate(SHIFTS):
        first = lax.rem(z + a, 4)
        for n in range(4):
            at = pl.multiple_of(first * 2048 + n * 512, 512)
            part = dot(inner, wdown[:, pl.ds(at, 512)])
            for t in range(4):
                stage[16 * i + 4 * n + t] = part[:, t * 128 : (t + 1) * 128]

        def pack_down(k, carry, i=i):
            dsib_out[8 * i + k] = stage[16 * i + 2 * k + 1 - core].astype(BF16)
            return carry

        lax.fori_loop(0, 8, pack_down, 0)
        group = pl.ds(8 * i, 8)
        exchange = to_sibling(
            dsib_out.at[group], dsib_in.at[group], dsib_send.at[i], dsib_recv.at[i]
        )
        exchange.start()
        exchanges.append(exchange)
    for i, a in enumerate(SHIFTS):
        exchanges[i].wait_recv()
        first = lax.rem(z + a, 4) * 8

        def send_down(k, carry, a=a, i=i, first=first):
            c = target(a, k)
            n = 8 * i + c - first
            total = stage[16 * i + 2 * (c - first) + core] + dsib_in[n].astype(F32)
            drs_out[n] = total.astype(BF16)
            remote(drs_out.at[n], drs_in.at[chip], rs_send.at[1], rs_recv.at[1], c).start()
            return carry

        lax.fori_loop(0, 8 if a else 7, send_down, 0)
    k = chip - z * 8
    drs_in[chip] = (stage[48 + 2 * k + core] + dsib_in[24 + k].astype(F32)).astype(BF16)
    done = remote(drs_out.at[part31], drs_in.at[part31], rs_send.at[1], rs_recv.at[1], chip)
    done.wait_recv()
    shares = lax.fori_loop(
        0, 32, lambda k, t: t + drs_in[k].astype(F32), jnp.zeros((64, 128), F32)
    )
    out_ref[...] = (residual.astype(F32) + shares).astype(BF16)
    done.wait_send()
    for exchange in exchanges:
        exchange.wait_send()


def local(
    hidden_in,
    attn_gain,
    w_query,
    key_value_weight,
    w_out,
    ffn_gain,
    w_gate,
    w_up,
    w_down,
    cached_key_slots,
    cached_value_slots,
    lengths,
    home_device,
    offset,
):
    vmem = pl.BlockSpec(memory_space=pltpu.VMEM)
    hbm = pl.BlockSpec(memory_space=pl.ANY)
    V = pltpu.VMEM
    dma = pltpu.SemaphoreType.DMA
    return pl.pallas_call(
        kernel,
        out_shape=jax.ShapeDtypeStruct((64, 128), BF16),
        in_specs=[hbm] * 14,
        out_specs=vmem,
        scratch_shapes=[
            V((64, 128), BF16),
            V((1, 128), BF16),
            V((8192,), BF16),
            V((1, 64), jnp.int32),
            V((1, 64), jnp.int32),
            V((1, 64), jnp.int32),
            V((64, 128), F32),
            V((128, 4096), BF16),
            V((128, 1024), BF16),
            V((4096, 128), BF16),
            V((8192, 256), BF16),
            V((8192, 256), BF16),
            V((256, 8192), BF16),
            V((SLOTS, 512), BF16),
            V((SLOTS, 512), BF16),
            V((64 * 48, 128), F32),
            V((8 * 48, 128), F32),
            V((32, 48, 128), BF16),
            V((32, 48, 128), BF16),
            V((32, 48, 128), BF16),
            V((32, 48, 128), BF16),
            V((8, 48, 128), BF16),
            V((8, 48, 128), BF16),
            V((64, 48, 128), BF16),
            V((SLOTS, 128), F32),
            V((64, 32, 128), BF16),
            V((8, 32, 128), BF16),
            V((8, 32, 128), BF16),
            V((64, 32, 128), BF16),
            V((64 * 32, 128), F32),
            V((256, 128), F32),
            V((80, 4096), BF16),
            V((64, 64, 128), BF16),
            V((64, 64, 128), F32),
            V((32, 64, 128), BF16),
            V((32, 64, 128), BF16),
            V((32, 64, 128), BF16),
            V((32, 64, 128), BF16),
            dma((8,)),
            dma((6,)),
            dma((4,)),
            dma((4,)),
            dma((2,)),
            dma((2,)),
            dma((2,)),
            dma((2,)),
            dma((4,)),
            dma((16,)),
            dma((16,)),
            dma((16,)),
            dma((4,)),
            dma((4,)),
        ],
        compiler_params=pltpu.CompilerParams(
            collective_id=0, has_side_effects=True, vmem_limit_bytes=60 << 20
        ),
    )(
        hidden_in,
        attn_gain.reshape(1, 128),
        ffn_gain,
        lengths.reshape(1, 64),
        home_device.reshape(1, 64),
        offset.reshape(1, 64),
        w_query,
        key_value_weight,
        w_out,
        w_gate,
        w_up,
        w_down,
        cached_key_slots,
        cached_value_slots,
    )


def solution(mesh):
    return jax.shard_map(
        local,
        mesh=mesh,
        in_specs=(
            P("unit", "pool"),
            P("pool"),
            P("pool", None),
            P("pool", None),
            P(None, "pool"),
            P(),
            P(None, "pool"),
            P(None, "pool"),
            P("pool", None),
            P(("unit", "pool"), None),
            P(("unit", "pool"), None),
            P("unit"),
            P("unit"),
            P("unit"),
        ),
        out_specs=P("unit", "pool"),
        check_vma=False,
    )
```

```python
import jax
import jax.numpy as jnp
from jax import lax
from jax.experimental import pallas as pl
from jax.experimental.pallas import tpu as pltpu
from jax.sharding import PartitionSpec as P

MESH = pl.DeviceIdType.MESH
F32 = jnp.float32
BF16 = jnp.bfloat16
EPSILON = 1e-05
MODEL = 8192
SLOTS = 5120
SCORE = 1024
MIX = 1024
SHIFTS = (2, 1, 3, 0)
EXTRA = 7


def dot(a, b):
    return jnp.dot(a, b, preferred_element_type=F32)


def iota(shape, axis):
    return lax.broadcasted_iota(jnp.int32, shape, axis)


def kernel(
    hidden_hbm,
    gain_hbm,
    ffn_gain_hbm,
    lengths_hbm,
    home_hbm,
    offset_hbm,
    wq_hbm,
    wkv_hbm,
    wout_hbm,
    wgate_hbm,
    wup_hbm,
    wdown_hbm,
    keys_hbm,
    values_hbm,
    out_ref,
    hidden_ref,
    gain_ref,
    ffn_gain_ref,
    lengths_ref,
    home_ref,
    offset_ref,
    gain_rows,
    wq,
    wkv,
    wout,
    wgate,
    wup,
    wdown,
    keys,
    values,
    blk,
    ext,
    sib_out,
    sib_in,
    rs_out,
    rs_in,
    xq_out,
    xq_in,
    xq_buf,
    scores,
    att_buf,
    xa_out,
    xa_in,
    xa_buf,
    spread,
    spread_extra,
    lhs,
    res_buf,
    stage,
    dsib_out,
    dsib_in,
    drs_out,
    drs_in,
    load_sem,
    small_sem,
    sib_send,
    sib_recv,
    ring_send,
    ring_recv,
    rs_send,
    rs_recv,
    ag_send,
    ag_recv,
    fwd_send,
    fwd_recv,
    dsib_send,
    dsib_recv,
):
    me = lax.axis_index("pool")
    chip = lax.div(me, 2)
    core = lax.rem(me, 2)
    z = lax.div(chip, 8)
    x = lax.rem(lax.div(chip, 2), 4)
    y = lax.rem(chip, 2)
    sibling = chip * 2 + (1 - core)
    my_slot = core * 32 + chip

    def target(a, k):
        b = 3 - lax.div(k, 2)
        e = 1 - lax.rem(k, 2)
        return lax.rem(z + a, 4) * 8 + lax.rem(x + b, 4) * 2 + lax.rem(y + e, 2)

    def each_chip(body):
        for a in SHIFTS:

            def step(k, carry, a=a):
                body(a, target(a, k))
                return carry

            lax.fori_loop(0, 8 if a else 7, step, 0)

    def remote(src, dst, send, recv, chip_to):
        return pltpu.make_async_remote_copy(
            src_ref=src,
            dst_ref=dst,
            send_sem=send,
            recv_sem=recv,
            device_id={"pool": chip_to * 2 + core},
            device_id_type=MESH,
        )

    def to_sibling(src, dst, send, recv):
        return pltpu.make_async_remote_copy(
            src_ref=src,
            dst_ref=dst,
            send_sem=send,
            recv_sem=recv,
            device_id={"pool": sibling},
            device_id_type=MESH,
        )

    member = x * 2 + core

    def ring_member(i):
        g = lax.rem(member + i, 8)
        return g, (z * 8 + lax.div(g, 2) * 2 + y) * 2 + lax.rem(g, 2)

    barrier = pltpu.get_barrier_semaphore()
    each_chip(
        lambda a, c: pl.semaphore_signal(
            barrier, inc=1, device_id={"pool": c * 2 + core}, device_id_type=MESH
        )
    )
    pl.semaphore_signal(barrier, inc=1, device_id={"pool": sibling}, device_id_type=MESH)
    for i in range(1, 4):
        other = (z * 8 + lax.rem(x + i, 4) * 2 + y) * 2 + 1 - core
        pl.semaphore_signal(barrier, inc=1, device_id={"pool": other}, device_id_type=MESH)

    loads = [
        pltpu.make_async_copy(src, dst, load_sem.at[i])
        for i, (src, dst) in enumerate(
            [
                (wq_hbm, wq),
                (wkv_hbm, wkv),
                (keys_hbm, keys),
                (values_hbm, values),
                (wout_hbm, wout),
                (wgate_hbm, wgate),
                (wup_hbm, wup),
                (wdown_hbm, wdown),
            ]
        )
    ]
    small = [
        pltpu.make_async_copy(src, dst, small_sem.at[i])
        for i, (src, dst) in enumerate(
            [
                (home_hbm, home_ref),
                (hidden_hbm, hidden_ref),
                (gain_hbm, gain_ref),
                (offset_hbm, offset_ref),
                (lengths_hbm, lengths_ref),
                (ffn_gain_hbm, ffn_gain_ref),
            ]
        )
    ]
    for load in small + loads[:2]:
        load.start()
    for load in small:
        load.wait()

    gain_rows[...] = ffn_gain_ref[...].reshape(64, 128).astype(F32)

    home_row = jnp.broadcast_to(home_ref[...].astype(F32), (64, 64))
    down_i = iota((64, 64), 0)
    along_i = iota((64, 64), 1)
    eye = down_i == along_i

    def column(row):
        return jnp.sum(jnp.where(eye, row, 0.0), axis=1, keepdims=True)

    home_col = column(home_row)
    same = jnp.where(home_col == home_row, 1.0, 0.0)
    rank_row = jnp.sum(jnp.where(down_i < along_i, same, 0.0), axis=0, keepdims=True)
    rank_col = jnp.sum(jnp.where(along_i < down_i, same, 0.0), axis=1, keepdims=True)
    extra_col = jnp.where(rank_col > 0.0, 1.0, 0.0)
    extra_row = jnp.where(rank_row > 0.0, 1.0, 0.0)
    order_row = jnp.sum(jnp.where(down_i < along_i, extra_col, 0.0), axis=0, keepdims=True)
    order_col = jnp.sum(jnp.where(along_i < down_i, extra_row, 0.0), axis=1, keepdims=True)
    half_row = jnp.floor(home_row[:1] * 0.5)
    half_col = jnp.floor(home_col * 0.5)
    slot_row = jnp.where(
        rank_row == 0.0, (home_row[:1] - 2.0 * half_row) * 32.0 + half_row, 64.0 + order_row
    )
    slot_col = jnp.where(
        rank_col == 0.0, (home_col - 2.0 * half_col) * 32.0 + half_col, 64.0 + order_col
    )
    to_slots = jnp.where(slot_row == iota((72, 64), 0).astype(F32), 1.0, 0.0).astype(BF16)
    from_slots = jnp.where(slot_col == iota((64, 80), 1).astype(F32), 1.0, 0.0).astype(BF16)
    here_row = home_row[:1] == me.astype(F32)
    here_col = home_col == me.astype(F32)
    lane = iota((1, 128), 1)
    lane_request = lax.div(lane, 32)
    offset_row = offset_ref[...].astype(F32)
    past_row = lengths_ref[...].astype(F32) - 1.0
    start = jnp.zeros((1, 128), F32)
    stop = jnp.zeros((1, 128), F32)
    for m in range(4):
        chosen = here_row & (rank_row == float(m))
        begin = jnp.sum(jnp.where(chosen, offset_row, 0.0), axis=1, keepdims=True)
        end = begin + jnp.sum(jnp.where(chosen, past_row, 0.0), axis=1, keepdims=True)
        start = jnp.where(lane_request == m, begin, start)
        stop = jnp.where(lane_request == m, end, stop)
    start = start.astype(jnp.int32)
    stop = stop.astype(jnp.int32)
    def floor_div(value, n):
        return jnp.floor((value + 0.5) * (1.0 / n))

    chunk_lane = iota((1, 384), 1).astype(F32)
    chunk_of = floor_div(chunk_lane, 48)
    chunk_row = chunk_lane - 48.0 * chunk_of
    extra_of = floor_div(chunk_row, 5)
    tile_of = 5.0 * chunk_of + chunk_row - 5.0 * extra_of
    in_lane = (order_col == extra_of) & (extra_col > 0.0)
    tile_row = iota((40, 384), 0).astype(F32)
    piece_down = iota((256, 1), 0)
    piece_extra = lax.rem(lax.div(piece_down, 4), 8).astype(F32)
    piece_head = (lax.div(piece_down, 32) * 4 + lax.rem(piece_down, 4)).astype(F32)
    in_piece = (order_row == piece_extra) & (extra_row > 0.0)
    head_lane = iota((256, 32), 1).astype(F32)
    pick_query, pick_att = [], []
    for m in range(1, 4):
        mine = jnp.where(here_col & (rank_col == float(m)), 1.0, 0.0)
        along = jnp.sum(jnp.where(in_lane, mine, 0.0), axis=0, keepdims=True)
        pick_query.append(jnp.where(tile_row == tile_of, along, 0.0))
        mine = jnp.where(here_row & (rank_row == float(m)), 1.0, 0.0)
        down = jnp.sum(jnp.where(in_piece, mine, 0.0), axis=1, keepdims=True)
        pick_att.append(jnp.where(head_lane == piece_head, down, 0.0))
    pick_query = jnp.concatenate(pick_query, axis=0).astype(BF16)
    pick_att = jnp.concatenate(pick_att, axis=1).astype(BF16)

    rows = dot(to_slots, hidden_ref[...])
    squares = jnp.sum(rows * rows, axis=1, keepdims=True)
    scaled = (rows * gain_ref[...].astype(F32)).astype(BF16)
    loads[0].wait()
    loads[1].wait()
    for load in loads[2:]:
        load.start()
    for n in range(10):
        weight = wq[:, n * 512 : (n + 1) * 512] if n < 8 else wkv[:, (n - 8) * 512 : (n - 7) * 512]
        part = dot(scaled, weight)
        for t in range(4):
            j = 4 * n + t
            tile = part[:, t * 128 : (t + 1) * 128]
            blk[pl.ds(j, 64, stride=48), :] = tile[:64]
            ext[pl.ds(48 * (j // 5) + j % 5, 8, stride=5), :] = tile[64:]
    for r in range(40, 48):
        if r != 45:
            blk[pl.ds(r, 64, stride=48), :] = jnp.zeros((64, 128), F32)

    def high_low(value, low):
        high = value.astype(BF16).astype(F32)
        return jnp.where(low, value - high, high)

    wide = jnp.broadcast_to(squares, (72, 128))
    blk[pl.ds(45, 64, stride=48), :] = high_low(wide[:64], iota((64, 128), 1) >= 64)
    extra_squares = jnp.where(lax.rem(iota((8, 128), 1), 64) == iota((8, 128), 0), wide[64:], 0.0)
    extra_squares = jnp.sum(extra_squares, axis=0, keepdims=True)
    extra_squares = high_low(extra_squares, lane >= 64)
    for g in range(8):
        ext[48 * g + 40 : 48 * g + 48, :] = jnp.zeros((8, 128), F32)
        ext[48 * g + 35 : 48 * g + 36, :] = extra_squares
        xq_out[g] = ext[48 * g : 48 * g + 48, :].astype(BF16)

    def block(slot):
        return blk[pl.ds(pl.multiple_of(slot * 48, 16), 48), :]

    def pack_sibling(k, carry):
        sib_out[k] = block((1 - core) * 32 + k).astype(BF16)
        return carry

    lax.fori_loop(0, 32, pack_sibling, 0, unroll=8)
    pl.semaphore_wait(barrier, 35)

    def ring_start(src, dst, p):
        def step(i, carry):
            g, device = ring_member(i)
            pltpu.make_async_remote_copy(
                src_ref=src.at[g],
                dst_ref=dst.at[member],
                send_sem=ring_send.at[p],
                recv_sem=ring_recv.at[p],
                device_id={"pool": device},
                device_id_type=MESH,
            ).start()
            return carry

        lax.fori_loop(1, 8, step, 0)
        dst[member] = src[member]

    def ring_end(src, dst, p):
        part7 = pl.ds(0, 7)
        done = to_sibling(src.at[part7], dst.at[part7], ring_send.at[p], ring_recv.at[p])
        done.wait()
        total = dst[0].astype(F32)
        for g in range(1, 8):
            total = total + dst[g].astype(F32)
        return total.astype(BF16)

    ring_start(xq_out, xq_in, 0)
    exchanges = []
    for i, a in enumerate(SHIFTS):
        group = pl.ds(lax.rem(z + a, 4) * 8, 8)
        exchange = to_sibling(sib_out.at[group], sib_in.at[group], sib_send.at[i], sib_recv.at[i])
        exchange.start()
        exchanges.append(exchange)

    def pack(k):
        rs_out[k] = (block(core * 32 + k) + sib_in[k].astype(F32)).astype(BF16)

    for i, a in enumerate(SHIFTS):
        exchanges[i].wait_recv()

        def send_sum(k, carry, a=a):
            c = target(a, k)
            pack(c)
            remote(rs_out.at[c], rs_in.at[chip], rs_send.at[0], rs_recv.at[0], c).start()
            return carry

        lax.fori_loop(0, 8 if a else 7, send_sum, 0)
    pack(chip)
    rs_in[chip] = rs_out[chip]

    def gather_start(buf, p):
        each_chip(
            lambda a, c: remote(
                buf.at[my_slot], buf.at[my_slot], ag_send.at[p], ag_recv.at[p * 4 + a], c
            ).start()
        )

    def gather_forward_one(buf, p, a):
        some = buf.at[pl.ds(0, 8 if a else 7)]
        remote(some, some, ag_send.at[p], ag_recv.at[p * 4 + a], chip).wait_recv()
        group = buf.at[pl.ds(core * 32 + lax.rem(z + 4 - a, 4) * 8, 8)]
        send = to_sibling(group, group, fwd_send.at[p * 4 + a], fwd_recv.at[p * 4 + a])
        send.start()
        return send

    def gather_forward(buf, p):
        return [gather_forward_one(buf, p, a) for a in SHIFTS]

    def gather_drain(buf, p):
        some = buf.at[pl.ds(0, 31)]
        remote(some, some, ag_send.at[p], ag_recv.at[p * 4], chip).wait_send()

    def gather_end(buf, p, sends):
        for send in sends:
            send.wait()
        gather_drain(buf, p)

    xq_buf[my_slot] = ring_end(xq_out, xq_in, 0)
    gather_start(xq_buf, 0)
    sends = gather_forward(xq_buf, 0)
    part31 = pl.ds(0, 31)
    done = remote(rs_out.at[part31], rs_in.at[part31], rs_send.at[0], rs_recv.at[0], chip)
    done.wait_recv()

    def add(k, total):
        return total + rs_in[k].astype(F32)

    summed = lax.fori_loop(0, 32, add, jnp.zeros((48, 128), F32), unroll=16)
    done.wait_send()
    for exchange in exchanges:
        exchange.wait_send()
    gather_end(xq_buf, 0, sends)

    def ring_total(buf, g, shape):
        first = (g % 2) * 32 + (g // 2) * 2

        def step(k, total):
            return total + buf[first + k * 8].astype(F32) + buf[first + k * 8 + 1].astype(F32)

        return lax.fori_loop(0, 4, step, jnp.zeros(shape, F32), unroll=True)

    own_squares = jnp.sum(summed[45:46], axis=1, keepdims=True) * (1.0 / 64.0)
    first = summed[:40] * lax.rsqrt(own_squares * (1.0 / MODEL) + EPSILON)
    pieces = [ring_total(xq_buf, g, (48, 128)) for g in range(8)]
    of_extra = lax.rem(iota((48, 128), 1), 64).astype(F32) == floor_div(
        iota((48, 128), 0).astype(F32), 5
    )
    extra_factor = jnp.sum(jnp.where(of_extra, pieces[0][35:36], 0.0), axis=1, keepdims=True)
    extra_factor = lax.rsqrt(extra_factor * (1.0 / MODEL) + EPSILON)
    extra_rows = jnp.concatenate([(p * extra_factor).astype(BF16) for p in pieces], axis=0)
    further = dot(pick_query, extra_rows)
    requests = [first] + [further[40 * m : 40 * (m + 1)] for m in range(3)]
    query = jnp.concatenate([r[:32] for r in requests], axis=0).astype(BF16).astype(F32)
    new_keys = jnp.concatenate([r[32:36] for r in requests], axis=0).astype(BF16)
    new_values = jnp.concatenate([r[36:40] for r in requests], axis=0).astype(BF16)
    query_t = query.T
    lane_head = lax.rem(lax.div(iota((128, 128), 1), 8), 4)
    spread_query = jnp.concatenate(
        [jnp.where(lane_head == k, query_t, 0.0) for k in range(4)], axis=0
    ).astype(BF16)
    scale = 128.0**-0.5
    own = dot(new_keys, query_t.astype(BF16)) * scale
    own = jnp.sum(
        jnp.where(lax.div(iota((16, 128), 1), 8) == iota((16, 128), 0), own, 0.0),
        axis=0,
        keepdims=True,
    )

    loads[2].wait()

    def score(i, best):
        at = pl.ds(pl.multiple_of(i * SCORE, SCORE), SCORE)
        s = dot(keys[at, :], spread_query) * scale
        slot = iota((SCORE, 128), 0) + i * SCORE
        s = jnp.where((slot >= start) & (slot < stop), s, -jnp.inf)
        scores[at, :] = s
        return jnp.maximum(best, jnp.max(s.reshape(SCORE // 8, 8, 128), axis=0))

    best = lax.fori_loop(0, SLOTS // SCORE, score, jnp.full((8, 128), -jnp.inf, F32), unroll=True)
    top = jnp.maximum(jnp.max(best, axis=0, keepdims=True), own)
    loads[3].wait()

    def mix(i, carry):
        total, mixed = carry
        at = pl.ds(pl.multiple_of(i * MIX, MIX), MIX)
        w = jnp.exp(scores[at, :] - top)
        total = total + jnp.sum(w.reshape(MIX // 8, 8, 128), axis=0)
        mixed = mixed + lax.dot_general(
            w.astype(BF16), values[at, :], (((0,), (0,)), ((), ())), preferred_element_type=F32
        )
        return total, mixed

    total, mixed = lax.fori_loop(
        0,
        SLOTS // MIX,
        mix,
        (jnp.zeros((8, 128), F32), jnp.zeros((128, 512), F32)),
        unroll=True,
    )
    own_weight = jnp.exp(own - top)
    total = jnp.sum(total, axis=0, keepdims=True) + own_weight
    eye128 = iota((128, 128), 0) == iota((128, 128), 1)
    total_col = jnp.sum(jnp.where(eye128, total, 0.0), axis=1, keepdims=True)
    own_col = jnp.sum(jnp.where(eye128, own_weight, 0.0), axis=1, keepdims=True)
    row_head = lax.rem(lax.div(iota((128, 128), 0), 8), 4)
    att = jnp.zeros((128, 128), F32)
    for k in range(4):
        att = jnp.where(row_head == k, mixed[:, k * 128 : (k + 1) * 128], att)
    own_spread = jnp.where(lax.div(iota((128, 16), 0), 8) == iota((128, 16), 1), own_col, 0.0)
    att = (att + dot(own_spread.astype(BF16), new_values)) / total_col

    att = att.astype(BF16)
    pieces = dot(pick_att, att[32:]).astype(BF16)
    for g in range(8):
        xa_out[g] = pieces[32 * g : 32 * (g + 1)]
    ring_start(xa_out, xa_in, 1)
    att_buf[my_slot] = att[:32]
    gather_start(att_buf, 1)
    xa_buf[my_slot] = ring_end(xa_out, xa_in, 1)
    gather_start(xa_buf, 3)
    sends = gather_forward(att_buf, 1)
    extra_sends = gather_forward(xa_buf, 3)
    gather_end(att_buf, 1, sends)

    def widen(s, carry):
        spread[pl.ds(pl.multiple_of(s * 32, 32), 32), :] = att_buf[s].astype(F32)
        return carry

    lax.fori_loop(0, 64, widen, 0, unroll=16)
    gather_end(xa_buf, 3, extra_sends)
    for g in range(8):
        spread_extra[32 * g : 32 * (g + 1), :] = ring_total(xa_buf, g, (32, 128))
    for h in range(32):
        at = slice(h * 128, (h + 1) * 128)
        lhs[:64, at] = spread[pl.ds(h, 64, stride=32), :].astype(BF16)
        lhs[64:, at] = jnp.concatenate(
            [spread_extra[pl.ds(32 * (h // 4) + h % 4, 8, stride=4), :], jnp.zeros((8, 128), F32)],
            axis=0,
        ).astype(BF16)
    loads[4].wait()
    projected = dot(lhs[...], wout[...])
    moved = jnp.zeros((64, 128), F32)
    for _ in range(3):
        piece = projected.astype(BF16)
        moved = moved + dot(from_slots, piece)
        projected = projected - piece.astype(F32)
    residual = (hidden_ref[...].astype(F32) + moved).astype(BF16)

    res_buf[my_slot] = residual
    gather_start(res_buf, 2)
    loads[5].wait()
    loads[6].wait()

    def hidden_units(a, parity, carry):
        def step(k, carry):
            squares, gate, up = carry
            some, gates, ups = [], [], []
            for n in range(2):
                c = lax.rem(z + 4 - a, 4) * 8 + 2 * k + n
                at = pl.ds(pl.multiple_of((2 * c + parity) * 128, 128), 128)
                value = res_buf[parity * 32 + c].astype(F32)
                squares = squares + value * value
                some.append((value * gain_rows[pl.ds(2 * c + parity, 1), :]).astype(BF16))
                gates.append(wgate[at, :])
                ups.append(wup[at, :])
            some = jnp.concatenate(some, axis=1)
            gate = gate + dot(some, jnp.concatenate(gates, axis=0))
            up = up + dot(some, jnp.concatenate(ups, axis=0))
            return squares, gate, up

        return lax.fori_loop(0, 4, step, carry, unroll=True)

    zero = jnp.zeros((64, 256), F32)
    carry = (jnp.zeros((64, 128), F32), zero, zero)
    sends = []
    for i, a in enumerate(SHIFTS):
        sends.append(gather_forward_one(res_buf, 2, a))
        carry = hidden_units(a, core, carry)
        if i:
            sends[i - 1].wait_recv()
            carry = hidden_units(SHIFTS[i - 1], 1 - core, carry)
    sends[3].wait_recv()
    squares, gate, up = hidden_units(SHIFTS[3], 1 - core, carry)
    gather_drain(res_buf, 2)
    for send in sends:
        send.wait_send()
    factor = lax.rsqrt(jnp.sum(squares, axis=1, keepdims=True) * (1.0 / MODEL) + EPSILON)
    gate = gate * factor
    inner = (gate / (1.0 + jnp.exp(-gate)) * (up * factor)).astype(BF16)

    loads[7].wait()
    exchanges = []
    for i, a in enumerate(SHIFTS):
        first = lax.rem(z + a, 4)
        for n in range(4):
            at = pl.multiple_of(first * 2048 + n * 512, 512)
            part = dot(inner, wdown[:, pl.ds(at, 512)])
            for t in range(4):
                stage[16 * i + 4 * n + t] = part[:, t * 128 : (t + 1) * 128]

        def pack_down(k, carry, i=i):
            dsib_out[8 * i + k] = stage[16 * i + 2 * k + 1 - core].astype(BF16)
            return carry

        lax.fori_loop(0, 8, pack_down, 0, unroll=True)
        group = pl.ds(8 * i, 8)
        exchange = to_sibling(
            dsib_out.at[group], dsib_in.at[group], dsib_send.at[i], dsib_recv.at[i]
        )
        exchange.start()
        exchanges.append(exchange)
    for i, a in enumerate(SHIFTS):
        exchanges[i].wait_recv()
        first = lax.rem(z + a, 4) * 8

        def send_down(k, carry, a=a, i=i, first=first):
            c = target(a, k)
            n = 8 * i + c - first
            total = stage[16 * i + 2 * (c - first) + core] + dsib_in[n].astype(F32)
            drs_out[n] = total.astype(BF16)
            remote(drs_out.at[n], drs_in.at[chip], rs_send.at[1], rs_recv.at[1], c).start()
            return carry

        lax.fori_loop(0, 8 if a else 7, send_down, 0)
    k = chip - z * 8
    drs_in[chip] = (stage[48 + 2 * k + core] + dsib_in[24 + k].astype(F32)).astype(BF16)
    done = remote(drs_out.at[part31], drs_in.at[part31], rs_send.at[1], rs_recv.at[1], chip)
    done.wait_recv()
    shares = lax.fori_loop(
        0, 32, lambda k, t: t + drs_in[k].astype(F32), jnp.zeros((64, 128), F32), unroll=16
    )
    out_ref[...] = (residual.astype(F32) + shares).astype(BF16)
    done.wait_send()
    for exchange in exchanges:
        exchange.wait_send()


def local(
    hidden_in,
    attn_gain,
    w_query,
    key_value_weight,
    w_out,
    ffn_gain,
    w_gate,
    w_up,
    w_down,
    cached_key_slots,
    cached_value_slots,
    lengths,
    home_device,
    offset,
):
    vmem = pl.BlockSpec(memory_space=pltpu.VMEM)
    hbm = pl.BlockSpec(memory_space=pl.ANY)
    V = pltpu.VMEM
    dma = pltpu.SemaphoreType.DMA
    return pl.pallas_call(
        kernel,
        out_shape=jax.ShapeDtypeStruct((64, 128), BF16),
        in_specs=[hbm] * 14,
        out_specs=vmem,
        scratch_shapes=[
            V((64, 128), BF16),
            V((1, 128), BF16),
            V((8192,), BF16),
            V((1, 64), jnp.int32),
            V((1, 64), jnp.int32),
            V((1, 64), jnp.int32),
            V((64, 128), F32),
            V((128, 4096), BF16),
            V((128, 1024), BF16),
            V((4096, 128), BF16),
            V((8192, 256), BF16),
            V((8192, 256), BF16),
            V((256, 8192), BF16),
            V((SLOTS, 512), BF16),
            V((SLOTS, 512), BF16),
            V((64 * 48, 128), F32),
            V((8 * 48, 128), F32),
            V((32, 48, 128), BF16),
            V((32, 48, 128), BF16),
            V((32, 48, 128), BF16),
            V((32, 48, 128), BF16),
            V((8, 48, 128), BF16),
            V((8, 48, 128), BF16),
            V((64, 48, 128), BF16),
            V((SLOTS, 128), F32),
            V((64, 32, 128), BF16),
            V((8, 32, 128), BF16),
            V((8, 32, 128), BF16),
            V((64, 32, 128), BF16),
            V((64 * 32, 128), F32),
            V((256, 128), F32),
            V((80, 4096), BF16),
            V((64, 64, 128), BF16),
            V((64, 64, 128), F32),
            V((32, 64, 128), BF16),
            V((32, 64, 128), BF16),
            V((32, 64, 128), BF16),
            V((32, 64, 128), BF16),
            dma((8,)),
            dma((6,)),
            dma((4,)),
            dma((4,)),
            dma((2,)),
            dma((2,)),
            dma((2,)),
            dma((2,)),
            dma((4,)),
            dma((16,)),
            dma((16,)),
            dma((16,)),
            dma((4,)),
            dma((4,)),
        ],
        compiler_params=pltpu.CompilerParams(
            collective_id=0, has_side_effects=True, vmem_limit_bytes=60 << 20
        ),
    )(
        hidden_in,
        attn_gain.reshape(1, 128),
        ffn_gain,
        lengths.reshape(1, 64),
        home_device.reshape(1, 64),
        offset.reshape(1, 64),
        w_query,
        key_value_weight,
        w_out,
        w_gate,
        w_up,
        w_down,
        cached_key_slots,
        cached_value_slots,
    )


def solution(mesh):
    return jax.shard_map(
        local,
        mesh=mesh,
        in_specs=(
            P("unit", "pool"),
            P("pool"),
            P("pool", None),
            P("pool", None),
            P(None, "pool"),
            P(),
            P(None, "pool"),
            P(None, "pool"),
            P("pool", None),
            P(("unit", "pool"), None),
            P(("unit", "pool"), None),
            P("unit"),
            P("unit"),
            P("unit"),
        ),
        out_specs=P("unit", "pool"),
        check_vma=False,
    )
```

```python
import jax
import jax.numpy as jnp
from jax import lax
from jax.experimental import pallas as pl
from jax.experimental.pallas import tpu as pltpu
from jax.sharding import PartitionSpec as P

MESH = pl.DeviceIdType.MESH
F32 = jnp.float32
BF16 = jnp.bfloat16
EPSILON = 1e-05
MODEL = 8192
SLOTS = 5120
SCORE = 1024
MIX = 1024
SHIFTS = (2, 1, 3, 0)
EXTRA = 7


def dot(a, b):
    return jnp.dot(a, b, preferred_element_type=F32)


def iota(shape, axis):
    return lax.broadcasted_iota(jnp.int32, shape, axis)


def kernel(
    hidden_hbm,
    gain_hbm,
    ffn_gain_hbm,
    lengths_hbm,
    home_hbm,
    offset_hbm,
    wq_hbm,
    wkv_hbm,
    wout_hbm,
    wgate_hbm,
    wup_hbm,
    wdown_hbm,
    keys_hbm,
    values_hbm,
    out_ref,
    hidden_ref,
    gain_ref,
    ffn_gain_ref,
    lengths_ref,
    home_ref,
    offset_ref,
    gain_rows,
    wq,
    wkv,
    wout,
    wgate,
    wup,
    wdown,
    keys,
    values,
    blk,
    ext,
    sib_out,
    sib_in,
    rs_out,
    rs_in,
    xq_out,
    xq_in,
    xq_buf,
    scores,
    att_buf,
    xa_out,
    xa_in,
    xa_buf,
    spread,
    spread_extra,
    lhs,
    res_buf,
    stage,
    dsib_out,
    dsib_in,
    drs_out,
    drs_in,
    load_sem,
    small_sem,
    sib_send,
    sib_recv,
    ring_send,
    ring_recv,
    rs_send,
    rs_recv,
    ag_send,
    ag_recv,
    fwd_send,
    fwd_recv,
    dsib_send,
    dsib_recv,
):
    me = lax.axis_index("pool")
    chip = lax.div(me, 2)
    core = lax.rem(me, 2)
    z = lax.div(chip, 8)
    x = lax.rem(lax.div(chip, 2), 4)
    y = lax.rem(chip, 2)
    sibling = chip * 2 + (1 - core)
    my_slot = core * 32 + chip

    def target(a, k):
        b = 3 - lax.div(k, 2)
        e = 1 - lax.rem(k, 2)
        return lax.rem(z + a, 4) * 8 + lax.rem(x + b, 4) * 2 + lax.rem(y + e, 2)

    def each_chip(body):
        for a in SHIFTS:

            def step(k, carry, a=a):
                body(a, target(a, k))
                return carry

            lax.fori_loop(0, 8 if a else 7, step, 0)

    def remote(src, dst, send, recv, chip_to):
        return pltpu.make_async_remote_copy(
            src_ref=src,
            dst_ref=dst,
            send_sem=send,
            recv_sem=recv,
            device_id={"pool": chip_to * 2 + core},
            device_id_type=MESH,
        )

    def to_sibling(src, dst, send, recv):
        return pltpu.make_async_remote_copy(
            src_ref=src,
            dst_ref=dst,
            send_sem=send,
            recv_sem=recv,
            device_id={"pool": sibling},
            device_id_type=MESH,
        )

    plane_member = lax.div(chip, 2) * 2 + core
    ring_of = x * 2 + core

    def plane(i):
        g = lax.rem(plane_member + i, 32)
        return g, (lax.div(g, 2) * 2 + y) * 2 + lax.rem(g, 2)

    def ring(i):
        g = lax.rem(ring_of + i, 8)
        return g, (z * 8 + lax.div(g, 2) * 2 + y) * 2 + lax.rem(g, 2)

    barrier = pltpu.get_barrier_semaphore()
    each_chip(
        lambda a, c: pl.semaphore_signal(
            barrier, inc=1, device_id={"pool": c * 2 + core}, device_id_type=MESH
        )
    )
    pl.semaphore_signal(barrier, inc=1, device_id={"pool": sibling}, device_id_type=MESH)

    def greet_plane(i, carry):
        other = (lax.rem(lax.div(chip, 2) + i, 16) * 2 + y) * 2 + 1 - core
        pl.semaphore_signal(barrier, inc=1, device_id={"pool": other}, device_id_type=MESH)
        return carry

    lax.fori_loop(1, 16, greet_plane, 0)

    loads = [
        pltpu.make_async_copy(src, dst, load_sem.at[i])
        for i, (src, dst) in enumerate(
            [
                (wq_hbm, wq),
                (wkv_hbm, wkv),
                (keys_hbm, keys),
                (values_hbm, values),
                (wout_hbm, wout),
                (wgate_hbm, wgate),
                (wup_hbm, wup),
                (wdown_hbm, wdown),
            ]
        )
    ]
    small = [
        pltpu.make_async_copy(src, dst, small_sem.at[i])
        for i, (src, dst) in enumerate(
            [
                (home_hbm, home_ref),
                (hidden_hbm, hidden_ref),
                (gain_hbm, gain_ref),
                (offset_hbm, offset_ref),
                (lengths_hbm, lengths_ref),
                (ffn_gain_hbm, ffn_gain_ref),
            ]
        )
    ]
    for load in small + loads[:2]:
        load.start()
    for load in small:
        load.wait()

    gain_rows[...] = ffn_gain_ref[...].reshape(64, 128).astype(F32)

    home_row = jnp.broadcast_to(home_ref[...].astype(F32), (64, 64))
    down_i = iota((64, 64), 0)
    along_i = iota((64, 64), 1)
    eye = down_i == along_i

    def column(row):
        return jnp.sum(jnp.where(eye, row, 0.0), axis=1, keepdims=True)

    home_col = column(home_row)
    same = jnp.where(home_col == home_row, 1.0, 0.0)
    rank_row = jnp.sum(jnp.where(down_i < along_i, same, 0.0), axis=0, keepdims=True)
    rank_col = jnp.sum(jnp.where(along_i < down_i, same, 0.0), axis=1, keepdims=True)
    extra_col = jnp.where(rank_col > 0.0, 1.0, 0.0)
    extra_row = jnp.where(rank_row > 0.0, 1.0, 0.0)
    order_row = jnp.sum(jnp.where(down_i < along_i, extra_col, 0.0), axis=0, keepdims=True)
    order_col = jnp.sum(jnp.where(along_i < down_i, extra_row, 0.0), axis=1, keepdims=True)
    half_row = jnp.floor(home_row[:1] * 0.5)
    half_col = jnp.floor(home_col * 0.5)
    slot_row = jnp.where(
        rank_row == 0.0, (home_row[:1] - 2.0 * half_row) * 32.0 + half_row, 64.0 + order_row
    )
    slot_col = jnp.where(
        rank_col == 0.0, (home_col - 2.0 * half_col) * 32.0 + half_col, 64.0 + order_col
    )
    to_slots = jnp.where(slot_row == iota((72, 64), 0).astype(F32), 1.0, 0.0).astype(BF16)
    from_slots = jnp.where(slot_col == iota((64, 80), 1).astype(F32), 1.0, 0.0).astype(BF16)
    here_row = home_row[:1] == me.astype(F32)
    here_col = home_col == me.astype(F32)
    lane = iota((1, 128), 1)
    lane_request = lax.div(lane, 32)
    offset_row = offset_ref[...].astype(F32)
    past_row = lengths_ref[...].astype(F32) - 1.0
    start = jnp.zeros((1, 128), F32)
    stop = jnp.zeros((1, 128), F32)
    for m in range(4):
        chosen = here_row & (rank_row == float(m))
        begin = jnp.sum(jnp.where(chosen, offset_row, 0.0), axis=1, keepdims=True)
        end = begin + jnp.sum(jnp.where(chosen, past_row, 0.0), axis=1, keepdims=True)
        start = jnp.where(lane_request == m, begin, start)
        stop = jnp.where(lane_request == m, end, stop)
    start = start.astype(jnp.int32)
    stop = stop.astype(jnp.int32)
    def floor_div(value, n):
        return jnp.floor((value + 0.5) * (1.0 / n))

    chunk_lane = iota((1, 512), 1)
    chunk_row = lax.rem(chunk_lane, 16).astype(F32)
    flat = lax.div(chunk_lane, 16).astype(F32) * 9.0 + chunk_row
    extra_of = floor_div(flat, 40)
    tile_of = flat - 40.0 * extra_of
    in_lane = (order_col == extra_of) & (extra_col > 0.0) & (chunk_row < 9.0)
    in_squares = (order_col == lax.rem(iota((64, 128), 1), 64).astype(F32)) & (extra_col > 0.0)
    tile_row = iota((40, 512), 0).astype(F32)
    piece_down = iota((256, 1), 0)
    piece_extra = lax.rem(lax.div(piece_down, 4), 8).astype(F32)
    piece_head = (lax.div(piece_down, 32) * 4 + lax.rem(piece_down, 4)).astype(F32)
    in_piece = (order_row == piece_extra) & (extra_row > 0.0)
    head_lane = iota((256, 32), 1).astype(F32)
    pick_query, pick_att, pick_squares = [], [], []
    for m in range(1, 4):
        mine = jnp.where(here_col & (rank_col == float(m)), 1.0, 0.0)
        along = jnp.sum(jnp.where(in_lane, mine, 0.0), axis=0, keepdims=True)
        pick_squares.append(
            jnp.sum(jnp.where(in_squares, mine, 0.0), axis=0, keepdims=True)
        )
        pick_query.append(jnp.where(tile_row == tile_of, along, 0.0))
        mine = jnp.where(here_row & (rank_row == float(m)), 1.0, 0.0)
        down = jnp.sum(jnp.where(in_piece, mine, 0.0), axis=1, keepdims=True)
        pick_att.append(jnp.where(head_lane == piece_head, down, 0.0))
    pick_query = jnp.concatenate(pick_query, axis=0).astype(BF16)
    pick_att = jnp.concatenate(pick_att, axis=1).astype(BF16)

    rows = dot(to_slots, hidden_ref[...])
    squares = jnp.sum(rows * rows, axis=1, keepdims=True)
    scaled = (rows * gain_ref[...].astype(F32)).astype(BF16)
    loads[0].wait()
    loads[1].wait()
    for load in loads[2:]:
        load.start()
    for n in range(10):
        weight = wq[:, n * 512 : (n + 1) * 512] if n < 8 else wkv[:, (n - 8) * 512 : (n - 7) * 512]
        part = dot(scaled, weight)
        for t in range(4):
            j = 4 * n + t
            tile = part[:, t * 128 : (t + 1) * 128]
            blk[pl.ds(j, 64, stride=48), :] = tile[:64]
            ext[pl.ds(j, 8, stride=40), :] = tile[64:]
    for r in range(40, 48):
        if r != 45:
            blk[pl.ds(r, 64, stride=48), :] = jnp.zeros((64, 128), F32)

    def high_low(value, low):
        high = value.astype(BF16).astype(F32)
        return jnp.where(low, value - high, high)

    wide = jnp.broadcast_to(squares, (72, 128))
    blk[pl.ds(45, 64, stride=48), :] = high_low(wide[:64], iota((64, 128), 1) >= 64)
    extra_squares = jnp.where(lax.rem(iota((8, 128), 1), 64) == iota((8, 128), 0), wide[64:], 0.0)
    extra_squares = jnp.sum(extra_squares, axis=0, keepdims=True)
    extra_squares = high_low(extra_squares, lane >= 64)
    for g in range(32):
        piece = jnp.where(iota((16, 128), 0) == 9, extra_squares, ext[9 * g : 9 * g + 16, :])
        xq_out[g] = piece.astype(BF16)

    def block(slot):
        return blk[pl.ds(pl.multiple_of(slot * 48, 16), 48), :]

    def pack_sibling(k, carry):
        sib_out[k] = block((1 - core) * 32 + k).astype(BF16)
        return carry

    lax.fori_loop(0, 32, pack_sibling, 0, unroll=8)
    pl.semaphore_wait(barrier, 47)

    def ring_start(src, dst, p, member, partner, n):
        def step(i, carry):
            g, device = partner(i)
            pltpu.make_async_remote_copy(
                src_ref=src.at[g],
                dst_ref=dst.at[member],
                send_sem=ring_send.at[p],
                recv_sem=ring_recv.at[p],
                device_id={"pool": device},
                device_id_type=MESH,
            ).start()
            return carry

        lax.fori_loop(1, n, step, 0)
        dst[member] = src[member]

    def ring_end(src, dst, p, n):
        rest = pl.ds(0, n - 1)
        done = to_sibling(src.at[rest], dst.at[rest], ring_send.at[p], ring_recv.at[p])
        done.wait()
        total = dst[0].astype(F32)
        for g in range(1, n):
            total = total + dst[g].astype(F32)
        return total.astype(BF16)

    ring_start(xq_out, xq_in, 0, plane_member, plane, 32)
    exchanges = []
    for i, a in enumerate(SHIFTS):
        group = pl.ds(lax.rem(z + a, 4) * 8, 8)
        exchange = to_sibling(sib_out.at[group], sib_in.at[group], sib_send.at[i], sib_recv.at[i])
        exchange.start()
        exchanges.append(exchange)

    def pack(k):
        rs_out[k] = (block(core * 32 + k) + sib_in[k].astype(F32)).astype(BF16)

    for i, a in enumerate(SHIFTS):
        exchanges[i].wait_recv()

        def send_sum(k, carry, a=a):
            c = target(a, k)
            pack(c)
            remote(rs_out.at[c], rs_in.at[chip], rs_send.at[0], rs_recv.at[0], c).start()
            return carry

        lax.fori_loop(0, 8 if a else 7, send_sum, 0)
    pack(chip)
    rs_in[chip] = rs_out[chip]

    def gather_start(buf, p):
        each_chip(
            lambda a, c: remote(
                buf.at[my_slot], buf.at[my_slot], ag_send.at[p], ag_recv.at[p * 4 + a], c
            ).start()
        )

    def gather_forward_one(buf, p, a):
        some = buf.at[pl.ds(0, 8 if a else 7)]
        remote(some, some, ag_send.at[p], ag_recv.at[p * 4 + a], chip).wait_recv()
        group = buf.at[pl.ds(core * 32 + lax.rem(z + 4 - a, 4) * 8, 8)]
        send = to_sibling(group, group, fwd_send.at[p * 4 + a], fwd_recv.at[p * 4 + a])
        send.start()
        return send

    def gather_forward(buf, p):
        return [gather_forward_one(buf, p, a) for a in SHIFTS]

    def gather_drain(buf, p):
        some = buf.at[pl.ds(0, 31)]
        remote(some, some, ag_send.at[p], ag_recv.at[p * 4], chip).wait_send()

    def gather_end(buf, p, sends):
        for send in sends:
            send.wait()
        gather_drain(buf, p)

    xq_buf[my_slot] = ring_end(xq_out, xq_in, 0, 32)
    gather_start(xq_buf, 0)
    sends = gather_forward(xq_buf, 0)
    part31 = pl.ds(0, 31)
    done = remote(rs_out.at[part31], rs_in.at[part31], rs_send.at[0], rs_recv.at[0], chip)
    done.wait_recv()

    def add(k, total):
        return total + rs_in[k].astype(F32)

    summed = lax.fori_loop(0, 32, add, jnp.zeros((48, 128), F32), unroll=16)
    done.wait_send()
    for exchange in exchanges:
        exchange.wait_send()
    gather_end(xq_buf, 0, sends)

    def ring_total(buf, g, shape):
        first = (g % 2) * 32 + (g // 2) * 2

        def step(k, total):
            return total + buf[first + k * 8].astype(F32) + buf[first + k * 8 + 1].astype(F32)

        return lax.fori_loop(0, 4, step, jnp.zeros(shape, F32), unroll=True)

    own_squares = jnp.sum(summed[45:46], axis=1, keepdims=True) * (1.0 / 64.0)
    first = summed[:40] * lax.rsqrt(own_squares * (1.0 / MODEL) + EPSILON)
    pieces = []
    for g in range(32):
        slot = (g % 2) * 32 + (g // 2) * 2
        pieces.append(xq_buf[slot].astype(F32) + xq_buf[slot + 1].astype(F32))
    extra_squares = pieces[0][9:10]
    rows = jnp.concatenate(pieces, axis=0)
    high = rows.astype(BF16)
    further = dot(pick_query, high) + dot(pick_query, (rows - high.astype(F32)).astype(BF16))
    factors = [
        lax.rsqrt(jnp.sum(p * extra_squares, axis=1, keepdims=True) * (1.0 / MODEL) + EPSILON)
        for p in pick_squares
    ]
    requests = [first] + [further[40 * m : 40 * (m + 1)] * factors[m] for m in range(3)]
    query = jnp.concatenate([r[:32] for r in requests], axis=0).astype(BF16).astype(F32)
    new_keys = jnp.concatenate([r[32:36] for r in requests], axis=0).astype(BF16)
    new_values = jnp.concatenate([r[36:40] for r in requests], axis=0).astype(BF16)
    query_t = query.T
    lane_head = lax.rem(lax.div(iota((128, 128), 1), 8), 4)
    spread_query = jnp.concatenate(
        [jnp.where(lane_head == k, query_t, 0.0) for k in range(4)], axis=0
    ).astype(BF16)
    scale = 128.0**-0.5
    own = dot(new_keys, query_t.astype(BF16)) * scale
    own = jnp.sum(
        jnp.where(lax.div(iota((16, 128), 1), 8) == iota((16, 128), 0), own, 0.0),
        axis=0,
        keepdims=True,
    )

    loads[2].wait()

    def score(i, best):
        at = pl.ds(pl.multiple_of(i * SCORE, SCORE), SCORE)
        s = dot(keys[at, :], spread_query) * scale
        slot = iota((SCORE, 128), 0) + i * SCORE
        s = jnp.where((slot >= start) & (slot < stop), s, -jnp.inf)
        scores[at, :] = s
        return jnp.maximum(best, jnp.max(s.reshape(SCORE // 8, 8, 128), axis=0))

    best = lax.fori_loop(0, SLOTS // SCORE, score, jnp.full((8, 128), -jnp.inf, F32), unroll=True)
    top = jnp.maximum(jnp.max(best, axis=0, keepdims=True), own)
    loads[3].wait()

    def mix(i, carry):
        total, mixed = carry
        at = pl.ds(pl.multiple_of(i * MIX, MIX), MIX)
        w = jnp.exp(scores[at, :] - top)
        total = total + jnp.sum(w.reshape(MIX // 8, 8, 128), axis=0)
        mixed = mixed + lax.dot_general(
            w.astype(BF16), values[at, :], (((0,), (0,)), ((), ())), preferred_element_type=F32
        )
        return total, mixed

    total, mixed = lax.fori_loop(
        0,
        SLOTS // MIX,
        mix,
        (jnp.zeros((8, 128), F32), jnp.zeros((128, 512), F32)),
        unroll=True,
    )
    own_weight = jnp.exp(own - top)
    total = jnp.sum(total, axis=0, keepdims=True) + own_weight
    eye128 = iota((128, 128), 0) == iota((128, 128), 1)
    total_col = jnp.sum(jnp.where(eye128, total, 0.0), axis=1, keepdims=True)
    own_col = jnp.sum(jnp.where(eye128, own_weight, 0.0), axis=1, keepdims=True)
    row_head = lax.rem(lax.div(iota((128, 128), 0), 8), 4)
    att = jnp.zeros((128, 128), F32)
    for k in range(4):
        att = jnp.where(row_head == k, mixed[:, k * 128 : (k + 1) * 128], att)
    own_spread = jnp.where(lax.div(iota((128, 16), 0), 8) == iota((128, 16), 1), own_col, 0.0)
    att = (att + dot(own_spread.astype(BF16), new_values)) / total_col

    att = att.astype(BF16)
    pieces = dot(pick_att, att[32:]).astype(BF16)
    for g in range(8):
        xa_out[g] = pieces[32 * g : 32 * (g + 1)]
    ring_start(xa_out, xa_in, 1, ring_of, ring, 8)
    att_buf[my_slot] = att[:32]
    gather_start(att_buf, 1)
    xa_buf[my_slot] = ring_end(xa_out, xa_in, 1, 8)
    gather_start(xa_buf, 3)
    sends = gather_forward(att_buf, 1)
    extra_sends = gather_forward(xa_buf, 3)
    gather_end(att_buf, 1, sends)

    def widen(s, carry):
        spread[pl.ds(pl.multiple_of(s * 32, 32), 32), :] = att_buf[s].astype(F32)
        return carry

    lax.fori_loop(0, 64, widen, 0, unroll=16)
    gather_end(xa_buf, 3, extra_sends)
    for g in range(8):
        spread_extra[32 * g : 32 * (g + 1), :] = ring_total(xa_buf, g, (32, 128))
    for h in range(32):
        at = slice(h * 128, (h + 1) * 128)
        lhs[:64, at] = spread[pl.ds(h, 64, stride=32), :].astype(BF16)
        lhs[64:, at] = jnp.concatenate(
            [spread_extra[pl.ds(32 * (h // 4) + h % 4, 8, stride=4), :], jnp.zeros((8, 128), F32)],
            axis=0,
        ).astype(BF16)
    loads[4].wait()
    projected = dot(lhs[...], wout[...])
    moved = jnp.zeros((64, 128), F32)
    for _ in range(3):
        piece = projected.astype(BF16)
        moved = moved + dot(from_slots, piece)
        projected = projected - piece.astype(F32)
    residual = (hidden_ref[...].astype(F32) + moved).astype(BF16)

    res_buf[my_slot] = residual
    gather_start(res_buf, 2)
    loads[5].wait()
    loads[6].wait()

    def hidden_units(a, parity, carry):
        def step(k, carry):
            squares, gate, up = carry
            some, gates, ups = [], [], []
            for n in range(2):
                c = lax.rem(z + 4 - a, 4) * 8 + 2 * k + n
                at = pl.ds(pl.multiple_of((2 * c + parity) * 128, 128), 128)
                value = res_buf[parity * 32 + c].astype(F32)
                squares = squares + value * value
                some.append((value * gain_rows[pl.ds(2 * c + parity, 1), :]).astype(BF16))
                gates.append(wgate[at, :])
                ups.append(wup[at, :])
            some = jnp.concatenate(some, axis=1)
            gate = gate + dot(some, jnp.concatenate(gates, axis=0))
            up = up + dot(some, jnp.concatenate(ups, axis=0))
            return squares, gate, up

        return lax.fori_loop(0, 4, step, carry, unroll=True)

    zero = jnp.zeros((64, 256), F32)
    carry = (jnp.zeros((64, 128), F32), zero, zero)
    sends = []
    for i, a in enumerate(SHIFTS):
        sends.append(gather_forward_one(res_buf, 2, a))
        carry = hidden_units(a, core, carry)
        if i:
            sends[i - 1].wait_recv()
            carry = hidden_units(SHIFTS[i - 1], 1 - core, carry)
    sends[3].wait_recv()
    squares, gate, up = hidden_units(SHIFTS[3], 1 - core, carry)
    gather_drain(res_buf, 2)
    for send in sends:
        send.wait_send()
    factor = lax.rsqrt(jnp.sum(squares, axis=1, keepdims=True) * (1.0 / MODEL) + EPSILON)
    gate = gate * factor
    inner = (gate / (1.0 + jnp.exp(-gate)) * (up * factor)).astype(BF16)

    loads[7].wait()
    exchanges = []
    for i, a in enumerate(SHIFTS):
        first = lax.rem(z + a, 4)
        for n in range(4):
            at = pl.multiple_of(first * 2048 + n * 512, 512)
            part = dot(inner, wdown[:, pl.ds(at, 512)])
            for t in range(4):
                stage[16 * i + 4 * n + t] = part[:, t * 128 : (t + 1) * 128]

        def pack_down(k, carry, i=i):
            dsib_out[8 * i + k] = stage[16 * i + 2 * k + 1 - core].astype(BF16)
            return carry

        lax.fori_loop(0, 8, pack_down, 0, unroll=True)
        group = pl.ds(8 * i, 8)
        exchange = to_sibling(
            dsib_out.at[group], dsib_in.at[group], dsib_send.at[i], dsib_recv.at[i]
        )
        exchange.start()
        exchanges.append(exchange)
    for i, a in enumerate(SHIFTS):
        exchanges[i].wait_recv()
        first = lax.rem(z + a, 4) * 8

        def send_down(k, carry, a=a, i=i, first=first):
            c = target(a, k)
            n = 8 * i + c - first
            total = stage[16 * i + 2 * (c - first) + core] + dsib_in[n].astype(F32)
            drs_out[n] = total.astype(BF16)
            remote(drs_out.at[n], drs_in.at[chip], rs_send.at[1], rs_recv.at[1], c).start()
            return carry

        lax.fori_loop(0, 8 if a else 7, send_down, 0)
    k = chip - z * 8
    drs_in[chip] = (stage[48 + 2 * k + core] + dsib_in[24 + k].astype(F32)).astype(BF16)
    done = remote(drs_out.at[part31], drs_in.at[part31], rs_send.at[1], rs_recv.at[1], chip)
    done.wait_recv()
    shares = lax.fori_loop(
        0, 32, lambda k, t: t + drs_in[k].astype(F32), jnp.zeros((64, 128), F32), unroll=16
    )
    out_ref[...] = (residual.astype(F32) + shares).astype(BF16)
    done.wait_send()
    for exchange in exchanges:
        exchange.wait_send()


def local(
    hidden_in,
    attn_gain,
    w_query,
    key_value_weight,
    w_out,
    ffn_gain,
    w_gate,
    w_up,
    w_down,
    cached_key_slots,
    cached_value_slots,
    lengths,
    home_device,
    offset,
):
    vmem = pl.BlockSpec(memory_space=pltpu.VMEM)
    hbm = pl.BlockSpec(memory_space=pl.ANY)
    V = pltpu.VMEM
    dma = pltpu.SemaphoreType.DMA
    return pl.pallas_call(
        kernel,
        out_shape=jax.ShapeDtypeStruct((64, 128), BF16),
        in_specs=[hbm] * 14,
        out_specs=vmem,
        scratch_shapes=[
            V((64, 128), BF16),
            V((1, 128), BF16),
            V((8192,), BF16),
            V((1, 64), jnp.int32),
            V((1, 64), jnp.int32),
            V((1, 64), jnp.int32),
            V((64, 128), F32),
            V((128, 4096), BF16),
            V((128, 1024), BF16),
            V((4096, 128), BF16),
            V((8192, 256), BF16),
            V((8192, 256), BF16),
            V((256, 8192), BF16),
            V((SLOTS, 512), BF16),
            V((SLOTS, 512), BF16),
            V((64 * 48, 128), F32),
            V((320, 128), F32),
            V((32, 48, 128), BF16),
            V((32, 48, 128), BF16),
            V((32, 48, 128), BF16),
            V((32, 48, 128), BF16),
            V((32, 16, 128), BF16),
            V((32, 16, 128), BF16),
            V((64, 16, 128), BF16),
            V((SLOTS, 128), F32),
            V((64, 32, 128), BF16),
            V((8, 32, 128), BF16),
            V((8, 32, 128), BF16),
            V((64, 32, 128), BF16),
            V((64 * 32, 128), F32),
            V((256, 128), F32),
            V((80, 4096), BF16),
            V((64, 64, 128), BF16),
            V((64, 64, 128), F32),
            V((32, 64, 128), BF16),
            V((32, 64, 128), BF16),
            V((32, 64, 128), BF16),
            V((32, 64, 128), BF16),
            dma((8,)),
            dma((6,)),
            dma((4,)),
            dma((4,)),
            dma((2,)),
            dma((2,)),
            dma((2,)),
            dma((2,)),
            dma((4,)),
            dma((16,)),
            dma((16,)),
            dma((16,)),
            dma((4,)),
            dma((4,)),
        ],
        compiler_params=pltpu.CompilerParams(
            collective_id=0, has_side_effects=True, vmem_limit_bytes=60 << 20
        ),
    )(
        hidden_in,
        attn_gain.reshape(1, 128),
        ffn_gain,
        lengths.reshape(1, 64),
        home_device.reshape(1, 64),
        offset.reshape(1, 64),
        w_query,
        key_value_weight,
        w_out,
        w_gate,
        w_up,
        w_down,
        cached_key_slots,
        cached_value_slots,
    )


def solution(mesh):
    return jax.shard_map(
        local,
        mesh=mesh,
        in_specs=(
            P("unit", "pool"),
            P("pool"),
            P("pool", None),
            P("pool", None),
            P(None, "pool"),
            P(),
            P(None, "pool"),
            P(None, "pool"),
            P("pool", None),
            P(("unit", "pool"), None),
            P(("unit", "pool"), None),
            P("unit"),
            P("unit"),
            P("unit"),
        ),
        out_specs=P("unit", "pool"),
        check_vma=False,
    )
```

```python
import jax
import jax.numpy as jnp
from jax import lax
from jax.experimental import pallas as pl
from jax.experimental.pallas import tpu as pltpu
from jax.sharding import PartitionSpec as P

MESH = pl.DeviceIdType.MESH
F32 = jnp.float32
BF16 = jnp.bfloat16
EPSILON = 1e-05
MODEL = 8192
SLOTS = 5120
SCORE = 1024
MIX = 1024
SHIFTS = (2, 1, 3, 0)
EXTRA = 7


def dot(a, b):
    return jnp.dot(a, b, preferred_element_type=F32)


def iota(shape, axis):
    return lax.broadcasted_iota(jnp.int32, shape, axis)


def kernel(
    hidden_hbm,
    gain_hbm,
    ffn_gain_hbm,
    lengths_hbm,
    home_hbm,
    offset_hbm,
    wq_hbm,
    wkv_hbm,
    wout_hbm,
    wgate_hbm,
    wup_hbm,
    wdown_hbm,
    keys_hbm,
    values_hbm,
    out_ref,
    hidden_ref,
    gain_ref,
    ffn_gain_ref,
    lengths_ref,
    home_ref,
    offset_ref,
    gain_rows,
    wq,
    wkv,
    wout,
    wgate,
    wup,
    wdown,
    keys,
    values,
    blk,
    ext,
    sib_out,
    sib_in,
    rs_out,
    rs_in,
    xq_out,
    xq_in,
    xq_buf,
    scores,
    att_buf,
    xa_out,
    xa_in,
    xa_buf,
    spread,
    spread_extra,
    lhs,
    res_buf,
    stage,
    dsib_out,
    dsib_in,
    drs_out,
    drs_in,
    load_sem,
    small_sem,
    sib_send,
    sib_recv,
    ring_send,
    ring_recv,
    rs_send,
    rs_recv,
    ag_send,
    ag_recv,
    fwd_send,
    fwd_recv,
    dsib_send,
    dsib_recv,
):
    me = lax.axis_index("pool")
    chip = lax.div(me, 2)
    core = lax.rem(me, 2)
    z = lax.div(chip, 8)
    x = lax.rem(lax.div(chip, 2), 4)
    y = lax.rem(chip, 2)
    sibling = chip * 2 + (1 - core)
    my_slot = core * 32 + chip

    def target(a, k):
        b = 3 - lax.div(k, 2)
        e = 1 - lax.rem(k, 2)
        return lax.rem(z + a, 4) * 8 + lax.rem(x + b, 4) * 2 + lax.rem(y + e, 2)

    def each_chip(body):
        for a in SHIFTS:

            def step(k, carry, a=a):
                body(a, target(a, k))
                return carry

            lax.fori_loop(0, 8 if a else 7, step, 0)

    def remote(src, dst, send, recv, chip_to):
        return pltpu.make_async_remote_copy(
            src_ref=src,
            dst_ref=dst,
            send_sem=send,
            recv_sem=recv,
            device_id={"pool": chip_to * 2 + core},
            device_id_type=MESH,
        )

    def to_sibling(src, dst, send, recv):
        return pltpu.make_async_remote_copy(
            src_ref=src,
            dst_ref=dst,
            send_sem=send,
            recv_sem=recv,
            device_id={"pool": sibling},
            device_id_type=MESH,
        )

    plane_member = lax.div(chip, 2) * 2 + core
    ring_of = x * 2 + core

    def plane(i):
        g = lax.rem(plane_member + i, 32)
        return g, (lax.div(g, 2) * 2 + y) * 2 + lax.rem(g, 2)

    def ring(i):
        g = lax.rem(ring_of + i, 8)
        return g, (z * 8 + lax.div(g, 2) * 2 + y) * 2 + lax.rem(g, 2)

    barrier = pltpu.get_barrier_semaphore()
    each_chip(
        lambda a, c: pl.semaphore_signal(
            barrier, inc=1, device_id={"pool": c * 2 + core}, device_id_type=MESH
        )
    )
    pl.semaphore_signal(barrier, inc=1, device_id={"pool": sibling}, device_id_type=MESH)

    def greet_plane(i, carry):
        other = (lax.rem(lax.div(chip, 2) + i, 16) * 2 + y) * 2 + 1 - core
        pl.semaphore_signal(barrier, inc=1, device_id={"pool": other}, device_id_type=MESH)
        return carry

    lax.fori_loop(1, 16, greet_plane, 0)

    loads = [
        pltpu.make_async_copy(src, dst, load_sem.at[i])
        for i, (src, dst) in enumerate(
            [
                (wq_hbm, wq),
                (wkv_hbm, wkv),
                (keys_hbm, keys),
                (values_hbm, values),
                (wout_hbm, wout),
                (wgate_hbm, wgate),
                (wup_hbm, wup),
                (wdown_hbm, wdown),
            ]
        )
    ]
    small = [
        pltpu.make_async_copy(src, dst, small_sem.at[i])
        for i, (src, dst) in enumerate(
            [
                (home_hbm, home_ref),
                (hidden_hbm, hidden_ref),
                (gain_hbm, gain_ref),
                (offset_hbm, offset_ref),
                (lengths_hbm, lengths_ref),
                (ffn_gain_hbm, ffn_gain_ref),
            ]
        )
    ]
    for load in small + loads[:2]:
        load.start()
    for load in small:
        load.wait()

    gain_rows[...] = ffn_gain_ref[...].reshape(64, 128).astype(F32)

    home_row = jnp.broadcast_to(home_ref[...].astype(F32), (64, 64))
    down_i = iota((64, 64), 0)
    along_i = iota((64, 64), 1)
    eye = down_i == along_i

    def column(row):
        return jnp.sum(jnp.where(eye, row, 0.0), axis=1, keepdims=True)

    home_col = column(home_row)
    same = jnp.where(home_col == home_row, 1.0, 0.0)
    rank_row = jnp.sum(jnp.where(down_i < along_i, same, 0.0), axis=0, keepdims=True)
    rank_col = jnp.sum(jnp.where(along_i < down_i, same, 0.0), axis=1, keepdims=True)
    extra_col = jnp.where(rank_col > 0.0, 1.0, 0.0)
    extra_row = jnp.where(rank_row > 0.0, 1.0, 0.0)
    order_row = jnp.sum(jnp.where(down_i < along_i, extra_col, 0.0), axis=0, keepdims=True)
    order_col = jnp.sum(jnp.where(along_i < down_i, extra_row, 0.0), axis=1, keepdims=True)
    half_row = jnp.floor(home_row[:1] * 0.5)
    half_col = jnp.floor(home_col * 0.5)
    slot_row = jnp.where(
        rank_row == 0.0, (home_row[:1] - 2.0 * half_row) * 32.0 + half_row, 64.0 + order_row
    )
    slot_col = jnp.where(
        rank_col == 0.0, (home_col - 2.0 * half_col) * 32.0 + half_col, 64.0 + order_col
    )
    to_slots = jnp.where(slot_row == iota((72, 64), 0).astype(F32), 1.0, 0.0).astype(BF16)
    from_slots = jnp.where(slot_col == iota((64, 80), 1).astype(F32), 1.0, 0.0).astype(BF16)
    here_row = home_row[:1] == me.astype(F32)
    here_col = home_col == me.astype(F32)
    lane = iota((1, 128), 1)
    lane_request = lax.div(lane, 32)
    offset_row = offset_ref[...].astype(F32)
    past_row = lengths_ref[...].astype(F32) - 1.0
    start = jnp.zeros((1, 128), F32)
    stop = jnp.zeros((1, 128), F32)
    for m in range(4):
        chosen = here_row & (rank_row == float(m))
        begin = jnp.sum(jnp.where(chosen, offset_row, 0.0), axis=1, keepdims=True)
        end = begin + jnp.sum(jnp.where(chosen, past_row, 0.0), axis=1, keepdims=True)
        start = jnp.where(lane_request == m, begin, start)
        stop = jnp.where(lane_request == m, end, stop)
    start = start.astype(jnp.int32)
    stop = stop.astype(jnp.int32)
    def floor_div(value, n):
        return jnp.floor((value + 0.5) * (1.0 / n))

    chunk_lane = iota((1, 512), 1)
    chunk_row = lax.rem(chunk_lane, 16).astype(F32)
    flat = lax.div(chunk_lane, 16).astype(F32) * 9.0 + chunk_row
    extra_of = floor_div(flat, 40)
    tile_of = flat - 40.0 * extra_of
    in_lane = (order_col == extra_of) & (extra_col > 0.0) & (chunk_row < 9.0)
    in_squares = (order_col == lax.rem(iota((64, 128), 1), 64).astype(F32)) & (extra_col > 0.0)
    tile_row = iota((40, 512), 0).astype(F32)
    piece_down = iota((256, 1), 0)
    piece_extra = lax.rem(lax.div(piece_down, 4), 8).astype(F32)
    piece_head = (lax.div(piece_down, 32) * 4 + lax.rem(piece_down, 4)).astype(F32)
    in_piece = (order_row == piece_extra) & (extra_row > 0.0)
    head_lane = iota((256, 32), 1).astype(F32)
    pick_query, pick_att, pick_squares = [], [], []
    for m in range(1, 4):
        mine = jnp.where(here_col & (rank_col == float(m)), 1.0, 0.0)
        along = jnp.sum(jnp.where(in_lane, mine, 0.0), axis=0, keepdims=True)
        pick_squares.append(
            jnp.sum(jnp.where(in_squares, mine, 0.0), axis=0, keepdims=True)
        )
        pick_query.append(jnp.where(tile_row == tile_of, along, 0.0))
        mine = jnp.where(here_row & (rank_row == float(m)), 1.0, 0.0)
        down = jnp.sum(jnp.where(in_piece, mine, 0.0), axis=1, keepdims=True)
        pick_att.append(jnp.where(head_lane == piece_head, down, 0.0))
    pick_query = jnp.concatenate(pick_query, axis=0).astype(BF16)
    pick_att = jnp.concatenate(pick_att, axis=1).astype(BF16)

    rows = dot(to_slots, hidden_ref[...])
    squares = jnp.sum(rows * rows, axis=1, keepdims=True)
    scaled = (rows * gain_ref[...].astype(F32)).astype(BF16)
    loads[0].wait()
    loads[1].wait()
    for load in loads[2:]:
        load.start()
    for n in range(10):
        weight = wq[:, n * 512 : (n + 1) * 512] if n < 8 else wkv[:, (n - 8) * 512 : (n - 7) * 512]
        part = dot(scaled, weight)
        for t in range(4):
            j = 4 * n + t
            tile = part[:, t * 128 : (t + 1) * 128]
            blk[pl.ds(j, 64, stride=48), :] = tile[:64]
            ext[pl.ds(j, 8, stride=40), :] = tile[64:]
    for r in range(40, 48):
        if r != 45:
            blk[pl.ds(r, 64, stride=48), :] = jnp.zeros((64, 128), F32)

    def high_low(value, low):
        high = value.astype(BF16).astype(F32)
        return jnp.where(low, value - high, high)

    wide = jnp.broadcast_to(squares, (72, 128))
    blk[pl.ds(45, 64, stride=48), :] = high_low(wide[:64], iota((64, 128), 1) >= 64)
    extra_squares = jnp.where(lax.rem(iota((8, 128), 1), 64) == iota((8, 128), 0), wide[64:], 0.0)
    extra_squares = jnp.sum(extra_squares, axis=0, keepdims=True)
    extra_squares = high_low(extra_squares, lane >= 64)
    for g in range(32):
        piece = jnp.where(iota((16, 128), 0) == 9, extra_squares, ext[9 * g : 9 * g + 16, :])
        xq_out[g] = piece.astype(BF16)

    def block(slot):
        return blk[pl.ds(pl.multiple_of(slot * 48, 16), 48), :]

    def pack_sibling(k, carry):
        sib_out[k] = block((1 - core) * 32 + k).astype(BF16)
        return carry

    lax.fori_loop(0, 32, pack_sibling, 0, unroll=8)
    pl.semaphore_wait(barrier, 47)

    def ring_start(src, dst, p, member, partner, n):
        def step(i, carry):
            g, device = partner(i)
            pltpu.make_async_remote_copy(
                src_ref=src.at[g],
                dst_ref=dst.at[member],
                send_sem=ring_send.at[p],
                recv_sem=ring_recv.at[p],
                device_id={"pool": device},
                device_id_type=MESH,
            ).start()
            return carry

        lax.fori_loop(1, n, step, 0)
        dst[member] = src[member]

    def ring_end(src, dst, p, n):
        rest = pl.ds(0, n - 1)
        done = to_sibling(src.at[rest], dst.at[rest], ring_send.at[p], ring_recv.at[p])
        done.wait()
        total = dst[0].astype(F32)
        for g in range(1, n):
            total = total + dst[g].astype(F32)
        return total.astype(BF16)

    ring_start(xq_out, xq_in, 0, plane_member, plane, 32)
    exchanges = []
    for i, a in enumerate(SHIFTS):
        group = pl.ds(lax.rem(z + a, 4) * 8, 8)
        exchange = to_sibling(sib_out.at[group], sib_in.at[group], sib_send.at[i], sib_recv.at[i])
        exchange.start()
        exchanges.append(exchange)

    def pack(k):
        rs_out[k] = (block(core * 32 + k) + sib_in[k].astype(F32)).astype(BF16)

    for i, a in enumerate(SHIFTS):
        exchanges[i].wait_recv()

        def send_sum(k, carry, a=a):
            c = target(a, k)
            pack(c)
            remote(rs_out.at[c], rs_in.at[chip], rs_send.at[0], rs_recv.at[0], c).start()
            return carry

        lax.fori_loop(0, 8 if a else 7, send_sum, 0, unroll=True)
    pack(chip)
    rs_in[chip] = rs_out[chip]

    def gather_start(buf, p):
        each_chip(
            lambda a, c: remote(
                buf.at[my_slot], buf.at[my_slot], ag_send.at[p], ag_recv.at[p * 4 + a], c
            ).start()
        )

    def gather_forward_one(buf, p, a):
        some = buf.at[pl.ds(0, 8 if a else 7)]
        remote(some, some, ag_send.at[p], ag_recv.at[p * 4 + a], chip).wait_recv()
        group = buf.at[pl.ds(core * 32 + lax.rem(z + 4 - a, 4) * 8, 8)]
        send = to_sibling(group, group, fwd_send.at[p * 4 + a], fwd_recv.at[p * 4 + a])
        send.start()
        return send

    def gather_forward(buf, p):
        return [gather_forward_one(buf, p, a) for a in SHIFTS]

    def gather_drain(buf, p):
        some = buf.at[pl.ds(0, 31)]
        remote(some, some, ag_send.at[p], ag_recv.at[p * 4], chip).wait_send()

    def gather_end(buf, p, sends):
        for send in sends:
            send.wait()
        gather_drain(buf, p)

    xq_buf[my_slot] = ring_end(xq_out, xq_in, 0, 32)
    gather_start(xq_buf, 0)
    sends = gather_forward(xq_buf, 0)
    part31 = pl.ds(0, 31)
    done = remote(rs_out.at[part31], rs_in.at[part31], rs_send.at[0], rs_recv.at[0], chip)
    done.wait_recv()

    def add(k, total):
        return total + rs_in[k].astype(F32)

    summed = lax.fori_loop(0, 32, add, jnp.zeros((48, 128), F32), unroll=16)
    done.wait_send()
    for exchange in exchanges:
        exchange.wait_send()
    gather_end(xq_buf, 0, sends)

    def ring_total(buf, g, shape):
        first = (g % 2) * 32 + (g // 2) * 2

        def step(k, total):
            return total + buf[first + k * 8].astype(F32) + buf[first + k * 8 + 1].astype(F32)

        return lax.fori_loop(0, 4, step, jnp.zeros(shape, F32), unroll=True)

    own_squares = jnp.sum(summed[45:46], axis=1, keepdims=True) * (1.0 / 64.0)
    first = summed[:40] * lax.rsqrt(own_squares * (1.0 / MODEL) + EPSILON)
    pieces = []
    for g in range(32):
        slot = (g % 2) * 32 + (g // 2) * 2
        pieces.append(xq_buf[slot].astype(F32) + xq_buf[slot + 1].astype(F32))
    extra_squares = pieces[0][9:10]
    rows = jnp.concatenate(pieces, axis=0)
    high = rows.astype(BF16)
    further = dot(pick_query, high) + dot(pick_query, (rows - high.astype(F32)).astype(BF16))
    factors = [
        lax.rsqrt(jnp.sum(p * extra_squares, axis=1, keepdims=True) * (1.0 / MODEL) + EPSILON)
        for p in pick_squares
    ]
    requests = [first] + [further[40 * m : 40 * (m + 1)] * factors[m] for m in range(3)]
    query = jnp.concatenate([r[:32] for r in requests], axis=0).astype(BF16).astype(F32)
    new_keys = jnp.concatenate([r[32:36] for r in requests], axis=0).astype(BF16)
    new_values = jnp.concatenate([r[36:40] for r in requests], axis=0).astype(BF16)
    query_t = query.T
    lane_head = lax.rem(lax.div(iota((128, 128), 1), 8), 4)
    spread_query = jnp.concatenate(
        [jnp.where(lane_head == k, query_t, 0.0) for k in range(4)], axis=0
    ).astype(BF16)
    scale = 128.0**-0.5
    own = dot(new_keys, query_t.astype(BF16)) * scale
    own = jnp.sum(
        jnp.where(lax.div(iota((16, 128), 1), 8) == iota((16, 128), 0), own, 0.0),
        axis=0,
        keepdims=True,
    )

    loads[2].wait()

    def score(i, best):
        at = pl.ds(pl.multiple_of(i * SCORE, SCORE), SCORE)
        s = dot(keys[at, :], spread_query) * scale
        slot = iota((SCORE, 128), 0) + i * SCORE
        s = jnp.where((slot >= start) & (slot < stop), s, -jnp.inf)
        scores[at, :] = s
        return jnp.maximum(best, jnp.max(s.reshape(SCORE // 8, 8, 128), axis=0))

    best = lax.fori_loop(0, SLOTS // SCORE, score, jnp.full((8, 128), -jnp.inf, F32), unroll=True)
    top = jnp.maximum(jnp.max(best, axis=0, keepdims=True), own)
    loads[3].wait()

    def mix(i, carry):
        total, mixed = carry
        at = pl.ds(pl.multiple_of(i * MIX, MIX), MIX)
        w = jnp.exp(scores[at, :] - top)
        total = total + jnp.sum(w.reshape(MIX // 8, 8, 128), axis=0)
        mixed = mixed + lax.dot_general(
            w.astype(BF16), values[at, :], (((0,), (0,)), ((), ())), preferred_element_type=F32
        )
        return total, mixed

    total, mixed = lax.fori_loop(
        0,
        SLOTS // MIX,
        mix,
        (jnp.zeros((8, 128), F32), jnp.zeros((128, 512), F32)),
        unroll=True,
    )
    own_weight = jnp.exp(own - top)
    total = jnp.sum(total, axis=0, keepdims=True) + own_weight
    eye128 = iota((128, 128), 0) == iota((128, 128), 1)
    total_col = jnp.sum(jnp.where(eye128, total, 0.0), axis=1, keepdims=True)
    own_col = jnp.sum(jnp.where(eye128, own_weight, 0.0), axis=1, keepdims=True)
    row_head = lax.rem(lax.div(iota((128, 128), 0), 8), 4)
    att = jnp.zeros((128, 128), F32)
    for k in range(4):
        att = jnp.where(row_head == k, mixed[:, k * 128 : (k + 1) * 128], att)
    own_spread = jnp.where(lax.div(iota((128, 16), 0), 8) == iota((128, 16), 1), own_col, 0.0)
    att = (att + dot(own_spread.astype(BF16), new_values)) / total_col

    att = att.astype(BF16)
    pieces = dot(pick_att, att[32:]).astype(BF16)
    for g in range(8):
        xa_out[g] = pieces[32 * g : 32 * (g + 1)]
    ring_start(xa_out, xa_in, 1, ring_of, ring, 8)
    att_buf[my_slot] = att[:32]
    gather_start(att_buf, 1)
    xa_buf[my_slot] = ring_end(xa_out, xa_in, 1, 8)
    gather_start(xa_buf, 3)
    sends = gather_forward(att_buf, 1)
    extra_sends = gather_forward(xa_buf, 3)
    gather_end(att_buf, 1, sends)

    def widen(s, carry):
        spread[pl.ds(pl.multiple_of(s * 32, 32), 32), :] = att_buf[s].astype(F32)
        return carry

    lax.fori_loop(0, 64, widen, 0, unroll=16)
    gather_end(xa_buf, 3, extra_sends)
    for g in range(8):
        spread_extra[32 * g : 32 * (g + 1), :] = ring_total(xa_buf, g, (32, 128))
    for h in range(32):
        at = slice(h * 128, (h + 1) * 128)
        lhs[:64, at] = spread[pl.ds(h, 64, stride=32), :].astype(BF16)
        lhs[64:, at] = jnp.concatenate(
            [spread_extra[pl.ds(32 * (h // 4) + h % 4, 8, stride=4), :], jnp.zeros((8, 128), F32)],
            axis=0,
        ).astype(BF16)
    loads[4].wait()
    projected = dot(lhs[...], wout[...])
    moved = jnp.zeros((64, 128), F32)
    for _ in range(3):
        piece = projected.astype(BF16)
        moved = moved + dot(from_slots, piece)
        projected = projected - piece.astype(F32)
    residual = (hidden_ref[...].astype(F32) + moved).astype(BF16)

    res_buf[my_slot] = residual
    gather_start(res_buf, 2)
    loads[5].wait()
    loads[6].wait()

    def hidden_units(a, parity, carry):
        def step(k, carry):
            squares, gate, up = carry
            some, gates, ups = [], [], []
            for n in range(2):
                c = lax.rem(z + 4 - a, 4) * 8 + 2 * k + n
                at = pl.ds(pl.multiple_of((2 * c + parity) * 128, 128), 128)
                value = res_buf[parity * 32 + c].astype(F32)
                squares = squares + value * value
                some.append((value * gain_rows[pl.ds(2 * c + parity, 1), :]).astype(BF16))
                gates.append(wgate[at, :])
                ups.append(wup[at, :])
            some = jnp.concatenate(some, axis=1)
            gate = gate + dot(some, jnp.concatenate(gates, axis=0))
            up = up + dot(some, jnp.concatenate(ups, axis=0))
            return squares, gate, up

        return lax.fori_loop(0, 4, step, carry, unroll=True)

    zero = jnp.zeros((64, 256), F32)
    carry = (jnp.zeros((64, 128), F32), zero, zero)
    sends = []
    for i, a in enumerate(SHIFTS):
        sends.append(gather_forward_one(res_buf, 2, a))
        carry = hidden_units(a, core, carry)
        if i:
            sends[i - 1].wait_recv()
            carry = hidden_units(SHIFTS[i - 1], 1 - core, carry)
    sends[3].wait_recv()
    squares, gate, up = hidden_units(SHIFTS[3], 1 - core, carry)
    gather_drain(res_buf, 2)
    for send in sends:
        send.wait_send()
    factor = lax.rsqrt(jnp.sum(squares, axis=1, keepdims=True) * (1.0 / MODEL) + EPSILON)
    gate = gate * factor
    inner = (gate / (1.0 + jnp.exp(-gate)) * (up * factor)).astype(BF16)

    loads[7].wait()
    exchanges = []
    for i, a in enumerate(SHIFTS):
        first = lax.rem(z + a, 4)
        for n in range(4):
            at = pl.multiple_of(first * 2048 + n * 512, 512)
            part = dot(inner, wdown[:, pl.ds(at, 512)])
            for t in range(4):
                stage[16 * i + 4 * n + t] = part[:, t * 128 : (t + 1) * 128]

        def pack_down(k, carry, i=i):
            dsib_out[8 * i + k] = stage[16 * i + 2 * k + 1 - core].astype(BF16)
            return carry

        lax.fori_loop(0, 8, pack_down, 0, unroll=True)
        group = pl.ds(8 * i, 8)
        exchange = to_sibling(
            dsib_out.at[group], dsib_in.at[group], dsib_send.at[i], dsib_recv.at[i]
        )
        exchange.start()
        exchanges.append(exchange)
    for i, a in enumerate(SHIFTS):
        exchanges[i].wait_recv()
        first = lax.rem(z + a, 4) * 8

        def send_down(k, carry, a=a, i=i, first=first):
            c = target(a, k)
            n = 8 * i + c - first
            total = stage[16 * i + 2 * (c - first) + core] + dsib_in[n].astype(F32)
            drs_out[n] = total.astype(BF16)
            remote(drs_out.at[n], drs_in.at[chip], rs_send.at[1], rs_recv.at[2 + a], c).start()
            return carry

        lax.fori_loop(0, 8 if a else 7, send_down, 0, unroll=True)
    k = chip - z * 8
    drs_in[chip] = (stage[48 + 2 * k + core] + dsib_in[24 + k].astype(F32)).astype(BF16)
    done = remote(drs_out.at[part31], drs_in.at[part31], rs_send.at[1], rs_recv.at[1], chip)
    shares = residual.astype(F32)
    for a in SHIFTS:
        some = pl.ds(0, 8 if a else 7)
        remote(
            drs_out.at[some], drs_in.at[some], rs_send.at[1], rs_recv.at[2 + a], chip
        ).wait_recv()
        first = lax.rem(z + 4 - a, 4) * 8
        for k in range(8):
            shares = shares + drs_in[first + k].astype(F32)
    out_ref[...] = shares.astype(BF16)
    done.wait_send()
    for exchange in exchanges:
        exchange.wait_send()


def local(
    hidden_in,
    attn_gain,
    w_query,
    key_value_weight,
    w_out,
    ffn_gain,
    w_gate,
    w_up,
    w_down,
    cached_key_slots,
    cached_value_slots,
    lengths,
    home_device,
    offset,
):
    vmem = pl.BlockSpec(memory_space=pltpu.VMEM)
    hbm = pl.BlockSpec(memory_space=pl.ANY)
    V = pltpu.VMEM
    dma = pltpu.SemaphoreType.DMA
    return pl.pallas_call(
        kernel,
        out_shape=jax.ShapeDtypeStruct((64, 128), BF16),
        in_specs=[hbm] * 14,
        out_specs=vmem,
        scratch_shapes=[
            V((64, 128), BF16),
            V((1, 128), BF16),
            V((8192,), BF16),
            V((1, 64), jnp.int32),
            V((1, 64), jnp.int32),
            V((1, 64), jnp.int32),
            V((64, 128), F32),
            V((128, 4096), BF16),
            V((128, 1024), BF16),
            V((4096, 128), BF16),
            V((8192, 256), BF16),
            V((8192, 256), BF16),
            V((256, 8192), BF16),
            V((SLOTS, 512), BF16),
            V((SLOTS, 512), BF16),
            V((64 * 48, 128), F32),
            V((320, 128), F32),
            V((32, 48, 128), BF16),
            V((32, 48, 128), BF16),
            V((32, 48, 128), BF16),
            V((32, 48, 128), BF16),
            V((32, 16, 128), BF16),
            V((32, 16, 128), BF16),
            V((64, 16, 128), BF16),
            V((SLOTS, 128), F32),
            V((64, 32, 128), BF16),
            V((8, 32, 128), BF16),
            V((8, 32, 128), BF16),
            V((64, 32, 128), BF16),
            V((64 * 32, 128), F32),
            V((256, 128), F32),
            V((80, 4096), BF16),
            V((64, 64, 128), BF16),
            V((64, 64, 128), F32),
            V((32, 64, 128), BF16),
            V((32, 64, 128), BF16),
            V((32, 64, 128), BF16),
            V((32, 64, 128), BF16),
            dma((8,)),
            dma((6,)),
            dma((4,)),
            dma((4,)),
            dma((2,)),
            dma((2,)),
            dma((2,)),
            dma((6,)),
            dma((4,)),
            dma((16,)),
            dma((16,)),
            dma((16,)),
            dma((4,)),
            dma((4,)),
        ],
        compiler_params=pltpu.CompilerParams(
            collective_id=0, has_side_effects=True, vmem_limit_bytes=60 << 20
        ),
    )(
        hidden_in,
        attn_gain.reshape(1, 128),
        ffn_gain,
        lengths.reshape(1, 64),
        home_device.reshape(1, 64),
        offset.reshape(1, 64),
        w_query,
        key_value_weight,
        w_out,
        w_gate,
        w_up,
        w_down,
        cached_key_slots,
        cached_value_slots,
    )


def solution(mesh):
    return jax.shard_map(
        local,
        mesh=mesh,
        in_specs=(
            P("unit", "pool"),
            P("pool"),
            P("pool", None),
            P("pool", None),
            P(None, "pool"),
            P(),
            P(None, "pool"),
            P(None, "pool"),
            P("pool", None),
            P(("unit", "pool"), None),
            P(("unit", "pool"), None),
            P("unit"),
            P("unit"),
            P("unit"),
        ),
        out_specs=P("unit", "pool"),
        check_vma=False,
    )
```
